512 devices in a mesh: pts: 64 (over y_lo, z, core), cen: 8 (over x, y_hi).
Axes of the slice: x: 4, y: 8 (y_hi: 2, y_lo: 4; y = y_hi * 4 + y_lo), z: 8, core: 2. Of those that a mesh axis runs over, the one named last changes fastest.
Arguments:
- points: bfloat16 [16384, 256], P('pts'), may hold values from -64 to 64
- centroids: bfloat16 [65536, 256], P('cen'), may hold values from -10 to 10
Outputs:
- updated: float32 [65536, 256], P(('cen', 'pts'))
- log_norm: float32 [16384], P('pts')
The draws below stay inside these ranges and needn't reach their ends.
All inputs are finite; a program needn't handle non-finite values.
Results may differ from the reference program's by a relative error of at most 0.0017.
Values may be sent and summed in bfloat16 or wider, within the bound.
No kernel may reach another device: no remote copies, remote signals or barrier semaphores. Data moves between devices by JAX's collectives and lax.ppermute only.
A program may use at most 64 MiB of HBM per device.

```python
import math
import jax
import jax.numpy as jnp
from jax import lax

D = 256
K = 65536
NPTS = 16384


def centroid_table(key):
    table = jnp.clip(jax.random.normal(jax.random.fold_in(key, 11), (K, D), jnp.float32), -6.0, 6.0)
    return table


def draw_centroids(key, part):
    return centroid_table(key).astype(jnp.bfloat16)


def draw_points(key, part):
    values = jnp.clip(jax.random.normal(jax.random.fold_in(key, 21), (NPTS, D), jnp.float32), -6.0, 6.0)
    return values.astype(jnp.bfloat16)


def setup_inputs(seed: int = 0) -> dict:
    keys = jax.random.split(jax.random.key(seed), 3)
    return {
        "points": draw_points(jax.random.fold_in(keys[2], 71), 0),
        "centroids": draw_centroids(jax.random.fold_in(keys[2], 71), 0),
    }


inv_temp = 0.0625
prior_count = 1.0


def reference(points, centroids):
    center_norms = jnp.sum(jnp.square(centroids.astype(jnp.float32)), axis=1)
    block_rows = math.gcd(NPTS, 1024)
    batches = points.reshape(NPTS // block_rows, block_rows, D)

    def one_block(totals, batch_rows):
        weighted, masses = totals
        logits = (2.0 * lax.dot_general(batch_rows, centroids, (((1,), (1,)), ((), ())), preferred_element_type=jnp.float32) - center_norms[None, :]) * inv_temp
        peak = jnp.max(logits, axis=1)
        row_log = peak + jnp.log(jnp.sum(jnp.exp(logits - peak[:, None]), axis=1))
        shares = jnp.exp(logits - row_log[:, None]).astype(jnp.bfloat16)
        weighted = weighted + lax.dot_general(shares, batch_rows, (((0,), (0,)), ((), ())), preferred_element_type=jnp.float32)
        masses = masses + jnp.sum(shares.astype(jnp.float32), axis=0)
        return (weighted, masses), row_log

    start = (jnp.zeros((K, D), jnp.float32), jnp.zeros((K,), jnp.float32))
    (weighted, masses), row_logs = lax.scan(one_block, start, batches)
    updated = (centroids.astype(jnp.float32) + weighted) / (prior_count + masses)[:, None]
    return updated, row_logs.reshape(NPTS)
```

```python
import jax
import jax.numpy as jnp
from jax import lax
from jax.experimental import pallas as pl
from jax.experimental.pallas import tpu as pltpu
from jax.sharding import Mesh
from jax.sharding import PartitionSpec as P

AXES = ("ya", "yb", "za", "zb", "co")
GATHER = ("yb", "zb", "co")
REDUCE = ("ya", "za")
CEN = "cen"
MIB = 1 << 20
inv_temp = 0.0625


def scores(table, rows):
    wide = table.astype(jnp.float32)
    norms = jnp.sum(wide * wide, axis=1, keepdims=True)
    products = lax.dot_general(
        table, rows, (((1,), (1,)), ((), ())), preferred_element_type=jnp.float32
    )
    return (2.0 * products - norms) * inv_temp


def first_kernel(table, rows, stats, peak, total):
    step = pl.program_id(0)

    @pl.when(step == 0)
    def _():
        peak[...] = jnp.full_like(peak, -jnp.inf)
        total[...] = jnp.zeros_like(total)

    logits = scores(table[...], rows[...])
    top = jnp.maximum(peak[...], jnp.max(logits, axis=0, keepdims=True))
    total[...] = total[...] * jnp.exp(peak[...] - top) + jnp.sum(
        jnp.exp(logits - top), axis=0, keepdims=True
    )
    peak[...] = top

    @pl.when(step == pl.num_programs(0) - 1)
    def _():
        stats[0:1, :] = peak[...]
        stats[1:2, :] = total[...]


def first_pass(points, centroids):
    n, d = points.shape
    k = centroids.shape[0]
    block = 1024
    return pl.pallas_call(
        first_kernel,
        grid=(k // block,),
        in_specs=[
            pl.BlockSpec((block, d), lambda i: (i, 0)),
            pl.BlockSpec((n, d), lambda i: (0, 0)),
        ],
        out_specs=pl.BlockSpec((2, n), lambda i: (0, 0)),
        out_shape=jax.ShapeDtypeStruct((2, n), jnp.float32),
        scratch_shapes=[pltpu.VMEM((1, n), jnp.float32)] * 2,
        compiler_params=pltpu.CompilerParams(vmem_limit_bytes=60 * MIB),
        cost_estimate=pl.CostEstimate(
            flops=2 * n * k * d, bytes_accessed=2 * k * d, transcendentals=n * k
        ),
        name="first_pass",
    )(centroids, points)


def second_kernel(place, stats, table, near, across, up, far, sums, log_norms):
    yb, zb = place[1], place[3]

    @pl.when(pl.program_id(0) == 0)
    def _():
        cen = stats.shape[0]
        peak = stats[0, :, 0, :]
        for c in range(1, cen):
            peak = jnp.maximum(peak, stats[c, :, 0, :])
        total = stats[0, :, 1, :] * jnp.exp(stats[0, :, 0, :] - peak)
        for c in range(1, cen):
            total = total + stats[c, :, 1, :] * jnp.exp(stats[c, :, 0, :] - peak)
        log_norms[...] = peak + jnp.log(total)

    _, owned, d = table.shape
    product = jnp.zeros((owned, d), jnp.float32)
    mass = jnp.zeros((8, owned), jnp.float32)
    pairs = ((near, yb, zb), (across, yb, 1 - zb), (up, 1 - yb, zb), (far, 1 - yb, 1 - zb))
    for rows, y, z in pairs:
        for c in range(2):
            logits = scores(table[0], rows[c])
            shift = log_norms[pl.ds((y * 2 + z) * 2 + c, 1), :]
            shares = jnp.exp(logits - shift).astype(jnp.bfloat16)
            product += lax.dot_general(
                shares, rows[c], (((1,), (0,)), ((), ())), preferred_element_type=jnp.float32
            )
            mass += lax.dot_general(
                jnp.ones((8, shares.shape[1]), jnp.bfloat16),
                shares,
                (((1,), (1,)), ((), ())),
                preferred_element_type=jnp.float32,
            )
    sums[0, :owned, :] = product
    sums[0, owned:, :] = jnp.concatenate([mass, jnp.zeros((8, d - owned), jnp.float32)], axis=1)


def second_pass(place, stats, table, blocks):
    reduced, owned, d = table.shape
    g, n = stats.shape[1], stats.shape[3]
    k = owned * reduced
    whole = pl.BlockSpec(blocks[0].shape, lambda i, place: (0, 0, 0))
    return pl.pallas_call(
        second_kernel,
        grid_spec=pltpu.PrefetchScalarGridSpec(
            num_scalar_prefetch=1,
            grid=(reduced,),
            in_specs=[
                pl.BlockSpec(stats.shape, lambda i, place: (0, 0, 0, 0)),
                pl.BlockSpec((1, owned, d), lambda i, place: (i, 0, 0)),
                *[whole] * 4,
            ],
            out_specs=[
                pl.BlockSpec((1, owned + 8, d), lambda i, place: (i, 0, 0)),
                pl.BlockSpec((g, n), lambda i, place: (0, 0)),
            ],
        ),
        out_shape=[
            jax.ShapeDtypeStruct((reduced, owned + 8, d), jnp.float32),
            jax.ShapeDtypeStruct((g, n), jnp.float32),
        ],
        compiler_params=pltpu.CompilerParams(vmem_limit_bytes=24 * MIB),
        cost_estimate=pl.CostEstimate(
            flops=4 * g * n * k * d, bytes_accessed=4 * k * d, transcendentals=g * n * k
        ),
        name="second_pass",
    )(place, stats, table, *blocks)


def last_kernel(place, parts, table, updated):
    owned = table.shape[1]
    total = parts[0]
    for r in range(1, parts.shape[0]):
        total = total + parts[r]
    mass = jnp.broadcast_to(total[owned : owned + 1, :owned], (owned, owned)).T
    for at in range(0, updated.shape[1], owned):
        here = slice(at, at + owned)
        updated[:, here] = (table[0, :, here].astype(jnp.float32) + total[:owned, here]) / (
            1.0 + mass
        )


def last_pass(place, parts, table):
    reduced, owned, d = table.shape

    def own(i, place):
        return (place[0] * (reduced // 2) + place[2], 0, 0)

    return pl.pallas_call(
        last_kernel,
        grid_spec=pltpu.PrefetchScalarGridSpec(
            num_scalar_prefetch=1,
            grid=(1,),
            in_specs=[
                pl.BlockSpec(parts.shape, lambda i, place: (0, 0, 0)),
                pl.BlockSpec((1, owned, d), own),
            ],
            out_specs=pl.BlockSpec((owned, d), lambda i, place: (0, 0)),
        ),
        out_shape=jax.ShapeDtypeStruct((owned, d), jnp.float32),
        compiler_params=pltpu.CompilerParams(vmem_limit_bytes=24 * MIB),
        name="last_pass",
    )(place, parts, table)


def body(points, centroids):
    n, d = points.shape
    cen = lax.axis_size(CEN)
    gathered = lax.axis_size(GATHER)
    reduced = lax.axis_size(REDUCE)
    owned = centroids.shape[0] // (gathered * reduced)
    place = jnp.stack([lax.axis_index(a) for a in AXES]).astype(jnp.int32)
    swap = [(0, 1), (1, 0)]

    near = lax.all_gather(points, "co")
    across = lax.ppermute(near, "zb", swap)
    up = lax.ppermute(near, "yb", swap)
    stats = first_pass(points, centroids)
    across, stats = lax.optimization_barrier((across, stats))
    far = lax.ppermute(across, "yb", swap)
    copies = jnp.broadcast_to(stats, (cen * gathered, 2, n))
    every = lax.all_to_all(copies, (CEN, *GATHER), 0, 0, tiled=True)
    every = every.reshape(cen, gathered, 2, n)
    sizes = [lax.axis_size(a) for a in AXES]
    at = (0, place[1], 0, place[3], place[4], 0, 0)
    cut = (sizes[0], 1, sizes[2], 1, 1, owned, d)
    table = lax.dynamic_slice(centroids.reshape(*sizes, owned, d), at, cut)
    table = table.reshape(reduced, owned, d)
    parts, log_norms = second_pass(place, every, table, (near, across, up, far))
    parts = lax.all_to_all(parts, REDUCE, 0, 0, tiled=True)
    updated = last_pass(place, parts, table)
    log_norm = lax.dynamic_slice_in_dim(log_norms, lax.axis_index(GATHER), 1, 0)[0]
    return updated, log_norm


def solution(mesh):
    shape = (2, 2, 4, 2, 2, mesh.shape["cen"])
    torus = Mesh(mesh.devices.reshape(shape), (*AXES, CEN))
    in_specs = (P(AXES, None), P(CEN, None))
    out_specs = (P((CEN, *AXES), None), P(AXES))
    return jax.shard_map(body, mesh=torus, in_specs=in_specs, out_specs=out_specs, check_vma=False)
```

```python
import jax
import jax.numpy as jnp
from jax import lax
from jax.experimental import pallas as pl
from jax.experimental.pallas import tpu as pltpu
from jax.sharding import Mesh
from jax.sharding import PartitionSpec as P

AXES = ("ya", "yb", "za", "zb", "co")
GATHER = ("yb", "zb", "co")
REDUCE = ("ya", "za")
CEN = "cen"
MIB = 1 << 20
CHUNK = 1024
inv_temp = 0.0625
SPAN, FLOOR = 240.0, 120.0


def squares(table):
    wide = table.astype(jnp.float32)
    return jnp.sum(wide * wide, axis=1, keepdims=True) * inv_temp


def products(table, rows):
    return lax.dot_general(
        table,
        rows * jnp.bfloat16(2.0 * inv_temp),
        (((1,), (1,)), ((), ())),
        preferred_element_type=jnp.float32,
    )


def first_kernel(centroids, rows, stats, table, arrived):
    chunks = table.shape[0] // CHUNK

    def copy(i):
        here = pl.ds(i * CHUNK, CHUNK)
        return pltpu.make_async_copy(centroids.at[here], table.at[here], arrived.at[i])

    for i in range(chunks):
        copy(i).start()

    def step(i, carry):
        peak, total = carry
        copy(i).wait()
        block = table[pl.ds(pl.multiple_of(i * CHUNK, CHUNK), CHUNK), :]
        logits = products(block, rows[...]) - squares(block)
        top = jnp.maximum(peak, jnp.max(logits, axis=0, keepdims=True))
        total = total * jnp.exp(peak - top) + jnp.sum(jnp.exp(logits - top), axis=0, keepdims=True)
        return top, total

    n = rows.shape[0]
    start = (jnp.full((1, n), -jnp.inf, jnp.float32), jnp.zeros((1, n), jnp.float32))
    peak, total = lax.fori_loop(0, chunks, step, start)
    stats[0:1, :] = peak
    stats[1:2, :] = total


def first_pass(points, centroids):
    n, d = points.shape
    k = centroids.shape[0]
    return pl.pallas_call(
        first_kernel,
        in_specs=[
            pl.BlockSpec(memory_space=pltpu.HBM),
            pl.BlockSpec(memory_space=pltpu.VMEM),
        ],
        out_specs=pl.BlockSpec(memory_space=pltpu.VMEM),
        out_shape=jax.ShapeDtypeStruct((2, n), jnp.float32),
        scratch_shapes=[
            pltpu.VMEM((k, d), centroids.dtype),
            pltpu.SemaphoreType.DMA((k // CHUNK,)),
        ],
        compiler_params=pltpu.CompilerParams(vmem_limit_bytes=20 * MIB),
        cost_estimate=pl.CostEstimate(
            flops=2 * n * k * d, bytes_accessed=2 * k * d, transcendentals=n * k
        ),
        name="first_pass",
    )(pltpu.with_memory_space_constraint(centroids, pltpu.HBM), points)


def second_kernel(stats, table, near, across, up, far, parts, own_norm, log_norms, sums, masses):
    yb, zb, co = (lax.axis_index(a) for a in GATHER)

    cen = stats.shape[0]
    peak = stats[0, :, 0, :]
    for c in range(1, cen):
        peak = jnp.maximum(peak, stats[c, :, 0, :])
    total = stats[0, :, 1, :] * jnp.exp(stats[0, :, 0, :] - peak)
    for c in range(1, cen):
        total = total + stats[c, :, 1, :] * jnp.exp(stats[c, :, 0, :] - peak)
    log_norms[...] = peak + jnp.log(total)
    own_norm[...] = log_norms[pl.ds((yb * 2 + zb) * 2 + co, 1), :]

    norms = squares(table[...])
    pairs = ((near, yb, zb), (across, yb, 1 - zb), (up, 1 - yb, zb), (far, 1 - yb, 1 - zb))
    for at, (rows, y, z) in enumerate(pairs):
        for c in range(2):
            shift = log_norms[pl.ds((y * 2 + z) * 2 + c, 1), :]
            logits = products(table[...], rows[c]) - norms
            shares = jnp.exp(logits - shift).astype(jnp.bfloat16)
            product = lax.dot_general(
                shares, rows[c], (((1,), (0,)), ((), ())), preferred_element_type=jnp.float32
            )
            wide = shares.astype(jnp.float32)
            mass = wide[:, :128] + wide[:, 128:]
            if at == 0 and c == 0:
                sums[...] = product
                masses[...] = mass
            else:
                sums[...] += product
                masses[...] += mass

    owned, d = parts.shape[1] - 16, parts.shape[2]
    line = lax.broadcasted_iota(jnp.int32, (16, d), 0)
    for r in range(parts.shape[0]):
        here = slice(r * owned, (r + 1) * owned)
        mass = masses[here, :]
        mean = sums[here, :] / (1.0 + jnp.sum(mass, axis=1, keepdims=True))
        size = jnp.abs(mean)
        scale = jnp.maximum(jnp.max(size, axis=0, keepdims=True) * 1.01, 1e-30)
        scale = scale.astype(jnp.bfloat16).astype(jnp.float32)
        code = jnp.exp2(size * (SPAN / scale) - FLOOR)
        parts[r, :owned, :] = jnp.where(mean < 0.0, -code, code).astype(jnp.bfloat16)
        mass = jnp.sum(mass.T, axis=0, keepdims=True)
        high = mass.astype(jnp.bfloat16).astype(jnp.float32)
        mid = (mass - high).astype(jnp.bfloat16).astype(jnp.float32)
        low = mass - high - mid
        upper = jnp.concatenate([high, mid], axis=1)
        lower = jnp.concatenate([low, jnp.zeros_like(low)], axis=1)
        tail = jnp.where(line == 0, scale, jnp.where(line == 1, upper, lower))
        parts[r, owned:, :] = tail.astype(jnp.bfloat16)


def second_pass(stats, table, blocks):
    reduced, owned, d = table.shape
    g, n = stats.shape[1], stats.shape[3]
    k = owned * reduced
    return pl.pallas_call(
        second_kernel,
        in_specs=[pl.BlockSpec(memory_space=pltpu.VMEM)] * 6,
        out_specs=[pl.BlockSpec(memory_space=pltpu.VMEM)] * 2,
        out_shape=[
            jax.ShapeDtypeStruct((reduced, owned + 16, d), jnp.bfloat16),
            jax.ShapeDtypeStruct((1, n), jnp.float32),
        ],
        scratch_shapes=[
            pltpu.VMEM((g, n), jnp.float32),
            pltpu.VMEM((k, d), jnp.float32),
            pltpu.VMEM((k, 128), jnp.float32),
        ],
        compiler_params=pltpu.CompilerParams(vmem_limit_bytes=24 * MIB),
        cost_estimate=pl.CostEstimate(
            flops=4 * g * n * k * d, bytes_accessed=4 * k * d, transcendentals=g * n * k
        ),
        name="second_pass",
    )(stats, table.reshape(k, d), *blocks)


def last_kernel(parts, table, updated):
    owned = updated.shape[0]
    own = table[lax.axis_index("ya") * lax.axis_size("za") + lax.axis_index("za")]
    sums = own.astype(jnp.float32)
    masses = jnp.ones((owned, owned), jnp.float32)
    for r in range(parts.shape[0]):
        tail = parts[r, owned:, :].astype(jnp.float32)
        mass = tail[1:2, :owned] + tail[1:2, owned:] + tail[2:3, :owned]
        mass = jnp.broadcast_to(mass, (owned, owned)).T
        code = parts[r, :owned, :].astype(jnp.float32)
        size = (jnp.log2(jnp.abs(code)) + FLOOR) * (tail[0:1, :] / SPAN)
        mean = jnp.where(code < 0.0, -size, size)
        weight = 1.0 + mass
        sums = sums + mean * jnp.concatenate([weight, weight], axis=1)
        masses = masses + mass
    updated[...] = sums / jnp.concatenate([masses, masses], axis=1)


def last_pass(parts, table):
    reduced, owned, d = table.shape
    return pl.pallas_call(
        last_kernel,
        in_specs=[pl.BlockSpec(memory_space=pltpu.VMEM)] * 2,
        out_specs=pl.BlockSpec(memory_space=pltpu.VMEM),
        out_shape=jax.ShapeDtypeStruct((owned, d), jnp.float32),
        compiler_params=pltpu.CompilerParams(vmem_limit_bytes=16 * MIB),
        name="last_pass",
    )(parts, table)


def body(points, centroids):
    n, d = points.shape
    cen = lax.axis_size(CEN)
    gathered = lax.axis_size(GATHER)
    reduced = lax.axis_size(REDUCE)
    owned = centroids.shape[0] // (gathered * reduced)
    swap = [(0, 1), (1, 0)]

    near = lax.all_gather(points, "co")
    across = lax.ppermute(near, "zb", swap)
    up = lax.ppermute(near, "yb", swap)
    stats = first_pass(points, centroids)
    copies = jnp.broadcast_to(stats, (cen * gathered, 2, n))
    across, copies = lax.optimization_barrier((across, copies))
    far = lax.ppermute(across, "yb", swap)
    every = lax.all_to_all(copies, (CEN, *GATHER), 0, 0, tiled=True)
    every = every.reshape(cen, gathered, 2, n)
    sizes = [lax.axis_size(a) for a in AXES]
    at = (0, lax.axis_index("yb"), 0, lax.axis_index("zb"), lax.axis_index("co"), 0, 0)
    cut = (sizes[0], 1, sizes[2], 1, 1, owned, d)
    table = lax.dynamic_slice(centroids.reshape(*sizes, owned, d), at, cut)
    table = table.reshape(reduced, owned, d)
    parts, log_norm = second_pass(every, table, (near, across, up, far))
    parts = lax.all_to_all(parts, REDUCE, 0, 0, tiled=True)
    return last_pass(parts, table), log_norm[0]


def solution(mesh):
    shape = (2, 2, 4, 2, 2, mesh.shape["cen"])
    torus = Mesh(mesh.devices.reshape(shape), (*AXES, CEN))
    in_specs = (P(AXES, None), P(CEN, None))
    out_specs = (P((CEN, *AXES), None), P(AXES))
    return jax.shard_map(body, mesh=torus, in_specs=in_specs, out_specs=out_specs, check_vma=False)
```

```python
import functools

import jax
import jax.numpy as jnp
from jax import lax
from jax.experimental import pallas as pl
from jax.experimental.pallas import tpu as pltpu
from jax.sharding import Mesh
from jax.sharding import PartitionSpec as P

AXES = ("yl", "z", "co")
CEN = ("x", "yh")
GATHER = ("yl", "co")
REDUCE = "z"
RING = ("yl", "yh")
MIB = 1 << 20
CHUNK = 1024
inv_temp = 0.0625
SPAN, FLOOR = 240.0, 120.0


def squares(table):
    wide = table.astype(jnp.float32)
    return jnp.sum(wide * wide, axis=1, keepdims=True) * inv_temp


def products(table, rows):
    return lax.dot_general(
        table,
        rows * jnp.bfloat16(2.0 * inv_temp),
        (((1,), (1,)), ((), ())),
        preferred_element_type=jnp.float32,
    )


def first_kernel(centroids, rows, stats, table, arrived):
    chunks = table.shape[0] // CHUNK

    def copy(i):
        here = pl.ds(i * CHUNK, CHUNK)
        return pltpu.make_async_copy(centroids.at[here], table.at[here], arrived.at[i])

    for i in range(chunks):
        copy(i).start()

    own = rows[lax.axis_index("co")]
    found = []
    for i in range(chunks):
        copy(i).wait()
        block = table[i * CHUNK : (i + 1) * CHUNK, :]
        logits = products(block, own) - squares(block)
        top = jnp.max(logits, axis=0, keepdims=True)
        found.append((top, jnp.sum(jnp.exp(logits - top), axis=0, keepdims=True)))
    peak = functools.reduce(jnp.maximum, [top for top, _ in found])
    total = sum(part * jnp.exp(top - peak) for top, part in found)
    stats[0:1, :] = peak
    stats[1:2, :] = total


def first_pass(near, centroids):
    _, n, d = near.shape
    k = centroids.shape[0]
    return pl.pallas_call(
        first_kernel,
        in_specs=[
            pl.BlockSpec(memory_space=pltpu.HBM),
            pl.BlockSpec(memory_space=pltpu.VMEM),
        ],
        out_specs=pl.BlockSpec(memory_space=pltpu.VMEM),
        out_shape=jax.ShapeDtypeStruct((2, n), jnp.float32),
        scratch_shapes=[
            pltpu.VMEM((k, d), centroids.dtype),
            pltpu.SemaphoreType.DMA((k // CHUNK,)),
        ],
        compiler_params=pltpu.CompilerParams(vmem_limit_bytes=20 * MIB),
        cost_estimate=pl.CostEstimate(
            flops=2 * n * k * d, bytes_accessed=2 * k * d, transcendentals=n * k
        ),
        name="first_pass",
    )(pltpu.with_memory_space_constraint(centroids, pltpu.HBM), near)


def second_kernel(stats, table, near, above, below, far, parts, own_norm, log_norms, sums, masses):
    yl, co = (lax.axis_index(a) for a in GATHER)

    cen = stats.shape[0]
    peak = stats[0, :, 0, :]
    for c in range(1, cen):
        peak = jnp.maximum(peak, stats[c, :, 0, :])
    total = stats[0, :, 1, :] * jnp.exp(stats[0, :, 0, :] - peak)
    for c in range(1, cen):
        total = total + stats[c, :, 1, :] * jnp.exp(stats[c, :, 0, :] - peak)
    log_norms[...] = peak + jnp.log(total)
    own_norm[...] = log_norms[pl.ds(yl * 2 + co, 1), :]

    norms = squares(table[...])
    pairs = ((near, 0), (below, 3), (above, 1), (far, 2))
    for at, (rows, off) in enumerate(pairs):
        for c in range(2):
            shift = log_norms[pl.ds(lax.rem(yl + off, 4) * 2 + c, 1), :]
            logits = products(table[...], rows[c]) - norms
            shares = jnp.exp(logits - shift).astype(jnp.bfloat16)
            product = lax.dot_general(
                shares, rows[c], (((1,), (0,)), ((), ())), preferred_element_type=jnp.float32
            )
            wide = shares.astype(jnp.float32)
            mass = wide[:, :128] + wide[:, 128:]
            if at == 0 and c == 0:
                sums[...] = product
                masses[...] = mass
            else:
                sums[...] += product
                masses[...] += mass

    owned, d = parts.shape[1] - 16, parts.shape[2]
    line = lax.broadcasted_iota(jnp.int32, (16, d), 0)
    for r in range(parts.shape[0]):
        here = slice(r * owned, (r + 1) * owned)
        mass = masses[here, :]
        mean = sums[here, :] / (1.0 + jnp.sum(mass, axis=1, keepdims=True))
        size = jnp.abs(mean)
        scale = jnp.maximum(jnp.max(size, axis=0, keepdims=True) * 1.01, 1e-30)
        scale = scale.astype(jnp.bfloat16).astype(jnp.float32)
        code = jnp.exp2(size * (SPAN / scale) - FLOOR)
        parts[r, :owned, :] = jnp.where(mean < 0.0, -code, code).astype(jnp.bfloat16)
        mass = jnp.sum(mass.T, axis=0, keepdims=True)
        high = mass.astype(jnp.bfloat16).astype(jnp.float32)
        mid = (mass - high).astype(jnp.bfloat16).astype(jnp.float32)
        low = mass - high - mid
        upper = jnp.concatenate([high, mid], axis=1)
        lower = jnp.concatenate([low, jnp.zeros_like(low)], axis=1)
        tail = jnp.where(line == 0, scale, jnp.where(line == 1, upper, lower))
        parts[r, owned:, :] = tail.astype(jnp.bfloat16)


def second_pass(stats, table, blocks):
    reduced, owned, d = table.shape
    g, n = stats.shape[1], stats.shape[3]
    k = owned * reduced
    return pl.pallas_call(
        second_kernel,
        in_specs=[pl.BlockSpec(memory_space=pltpu.VMEM)] * 6,
        out_specs=[pl.BlockSpec(memory_space=pltpu.VMEM)] * 2,
        out_shape=[
            jax.ShapeDtypeStruct((reduced, owned + 16, d), jnp.bfloat16),
            jax.ShapeDtypeStruct((1, n), jnp.float32),
        ],
        scratch_shapes=[
            pltpu.VMEM((g, n), jnp.float32),
            pltpu.VMEM((k, d), jnp.float32),
            pltpu.VMEM((k, 128), jnp.float32),
        ],
        compiler_params=pltpu.CompilerParams(vmem_limit_bytes=24 * MIB),
        cost_estimate=pl.CostEstimate(
            flops=4 * g * n * k * d, bytes_accessed=4 * k * d, transcendentals=g * n * k
        ),
        name="second_pass",
    )(stats, table.reshape(k, d), *blocks)


def last_kernel(parts, table, updated):
    owned = updated.shape[0]
    own = table[lax.axis_index(REDUCE)]
    sums = own.astype(jnp.float32)
    masses = jnp.ones((owned, owned), jnp.float32)
    for r in range(parts.shape[0]):
        tail = parts[r, owned:, :].astype(jnp.float32)
        mass = tail[1:2, :owned] + tail[1:2, owned:] + tail[2:3, :owned]
        mass = jnp.broadcast_to(mass, (owned, owned)).T
        code = parts[r, :owned, :].astype(jnp.float32)
        size = (jnp.log2(jnp.abs(code)) + FLOOR) * (tail[0:1, :] / SPAN)
        mean = jnp.where(code < 0.0, -size, size)
        weight = 1.0 + mass
        sums = sums + mean * jnp.concatenate([weight, weight], axis=1)
        masses = masses + mass
    updated[...] = sums / jnp.concatenate([masses, masses], axis=1)


def last_pass(parts, table):
    reduced, owned, d = table.shape
    return pl.pallas_call(
        last_kernel,
        in_specs=[pl.BlockSpec(memory_space=pltpu.VMEM)] * 2,
        out_specs=pl.BlockSpec(memory_space=pltpu.VMEM),
        out_shape=jax.ShapeDtypeStruct((owned, d), jnp.float32),
        compiler_params=pltpu.CompilerParams(vmem_limit_bytes=16 * MIB),
        name="last_pass",
    )(parts, table)


def moved(array, hops):
    low, high = (lax.axis_size(a) for a in RING)
    place = [(y % low) * high + y // low for y in range(low * high)]
    pairs = [(place[y], place[(y + hops) % (low * high)]) for y in range(low * high)]
    return lax.ppermute(array, RING, pairs)


def body(points, centroids):
    n, d = points.shape
    cen = lax.axis_size(CEN)
    gathered = lax.axis_size(GATHER)
    reduced = lax.axis_size(REDUCE)
    owned = centroids.shape[0] // (gathered * reduced)

    near = lax.all_gather(points, "co")
    below, above, far = moved(near, 1), moved(near, -1), moved(near, 2)
    stats = first_pass(near, centroids)
    copies = jnp.broadcast_to(stats, (cen * gathered, 2, n))
    every = lax.all_to_all(copies, (*CEN, *GATHER), 0, 0, tiled=True)
    every = every.reshape(cen, gathered, 2, n)
    sizes = [lax.axis_size(a) for a in AXES]
    at = (lax.axis_index("yl"), 0, lax.axis_index("co"), 0, 0)
    table = lax.dynamic_slice(
        centroids.reshape(*sizes, owned, d), at, (1, reduced, 1, owned, d)
    )
    table = lax.optimization_barrier(table.reshape(reduced, owned, d))
    parts, log_norm = second_pass(every, table, (near, above, below, far))
    parts = lax.all_to_all(parts, REDUCE, 0, 0, tiled=True)
    return last_pass(parts, table), log_norm[0]


def solution(mesh):
    torus = Mesh(mesh.devices.reshape(4, 8, 2, 4, 2), (*AXES, *CEN))
    in_specs = (P(AXES, None), P(CEN, None))
    out_specs = (P((*CEN, *AXES), None), P(AXES))
    return jax.shard_map(body, mesh=torus, in_specs=in_specs, out_specs=out_specs, check_vma=False)
```

```python
import jax
import jax.numpy as jnp
from jax import lax
from jax.experimental import pallas as pl
from jax.experimental.pallas import tpu as pltpu
from jax.sharding import Mesh
from jax.sharding import PartitionSpec as P

AXES = ("yl", "z", "co")
CEN = ("x", "yh")
GATHER = ("yl", "co")
REDUCE = "z"
RING = ("yl", "co", "yh")
MIB = 1 << 20
CHUNK = 2048
inv_temp = 0.0625
SPAN, FLOOR = 240.0, 120.0


def squares(table):
    wide = table.astype(jnp.float32)
    return jnp.sum(wide * wide, axis=1, keepdims=True) * inv_temp


def products(table, rows):
    return lax.dot_general(
        table,
        rows * jnp.bfloat16(2.0 * inv_temp),
        (((1,), (1,)), ((), ())),
        preferred_element_type=jnp.float32,
    )


def first_kernel(centroids, points, stats, table, rows, arrived, ready):
    chunks = table.shape[0] // CHUNK

    def copy(i):
        here = pl.ds(i * CHUNK, CHUNK)
        return pltpu.make_async_copy(centroids.at[here], table.at[here], arrived.at[i])

    own = pltpu.make_async_copy(points, rows, ready)
    own.start()
    for i in range(chunks):
        copy(i).start()
    own.wait()

    def step(i, carry):
        peak, total = carry
        copy(i).wait()
        block = table[pl.ds(pl.multiple_of(i * CHUNK, CHUNK), CHUNK), :]
        logits = products(block, rows[...]) - squares(block)
        top = jnp.maximum(peak, jnp.max(logits, axis=0, keepdims=True))
        total = total * jnp.exp(peak - top) + jnp.sum(jnp.exp(logits - top), axis=0, keepdims=True)
        return top, total

    n = rows.shape[0]
    start = (jnp.full((1, n), -jnp.inf, jnp.float32), jnp.zeros((1, n), jnp.float32))
    peak, total = lax.fori_loop(0, chunks, step, start)
    both = jnp.concatenate([peak, total], axis=0)
    for i in range(stats.shape[0]):
        stats[i] = both


def first_pass(points, centroids, receivers):
    n, d = points.shape
    k = centroids.shape[0]
    return pl.pallas_call(
        first_kernel,
        in_specs=[pl.BlockSpec(memory_space=pltpu.HBM)] * 2,
        out_specs=pl.BlockSpec(memory_space=pltpu.VMEM),
        out_shape=jax.ShapeDtypeStruct((receivers, 2, n), jnp.float32),
        scratch_shapes=[
            pltpu.VMEM((k, d), centroids.dtype),
            pltpu.VMEM((n, d), points.dtype),
            pltpu.SemaphoreType.DMA((k // CHUNK,)),
            pltpu.SemaphoreType.DMA,
        ],
        compiler_params=pltpu.CompilerParams(vmem_limit_bytes=24 * MIB),
        cost_estimate=pl.CostEstimate(
            flops=2 * n * k * d, bytes_accessed=2 * k * d, transcendentals=n * k
        ),
        name="first_pass",
    )(*(pltpu.with_memory_space_constraint(a, pltpu.HBM) for a in (centroids, points)))


def second_kernel(stats, table, near, sides, far, parts, own_norm, log_norms, sums, masses):
    yl, co = (lax.axis_index(a) for a in GATHER)

    cen = stats.shape[0]
    peak = stats[0, :, 0, :]
    for c in range(1, cen):
        peak = jnp.maximum(peak, stats[c, :, 0, :])
    total = stats[0, :, 1, :] * jnp.exp(stats[0, :, 0, :] - peak)
    for c in range(1, cen):
        total = total + stats[c, :, 1, :] * jnp.exp(stats[c, :, 0, :] - peak)
    log_norms[...] = peak + jnp.log(total)
    own_norm[...] = log_norms[pl.ds(yl * 2 + co, 1), :]

    norms = squares(table[...])
    pairs = ((near, 0), (sides.at[0], 3), (sides.at[1], 1), (far, 2))
    for at, (rows, off) in enumerate(pairs):
        for c in range(2):
            shift = log_norms[pl.ds(lax.rem(yl + off, 4) * 2 + c, 1), :]
            logits = products(table[...], rows[c]) - norms
            shares = jnp.exp(logits - shift).astype(jnp.bfloat16)
            product = lax.dot_general(
                shares, rows[c], (((1,), (0,)), ((), ())), preferred_element_type=jnp.float32
            )
            wide = shares.astype(jnp.float32)
            mass = wide[:, :128] + wide[:, 128:]
            if at == 0 and c == 0:
                sums[...] = product
                masses[...] = mass
            else:
                sums[...] += product
                masses[...] += mass

    owned, d = parts.shape[1] - 16, parts.shape[2]
    line = lax.broadcasted_iota(jnp.int32, (16, d), 0)
    for r in range(parts.shape[0]):
        here = slice(r * owned, (r + 1) * owned)
        mass = masses[here, :]
        mean = sums[here, :] / (1.0 + jnp.sum(mass, axis=1, keepdims=True))
        size = jnp.abs(mean)
        scale = jnp.maximum(jnp.max(size, axis=0, keepdims=True) * 1.01, 1e-30)
        scale = scale.astype(jnp.bfloat16).astype(jnp.float32)
        code = jnp.exp2(size * (SPAN / scale) - FLOOR)
        parts[r, :owned, :] = jnp.where(mean < 0.0, -code, code).astype(jnp.bfloat16)
        mass = jnp.sum(mass.T, axis=0, keepdims=True)
        high = mass.astype(jnp.bfloat16).astype(jnp.float32)
        mid = (mass - high).astype(jnp.bfloat16).astype(jnp.float32)
        low = mass - high - mid
        upper = jnp.concatenate([high, mid], axis=1)
        lower = jnp.concatenate([low, jnp.zeros_like(low)], axis=1)
        tail = jnp.where(line == 0, scale, jnp.where(line == 1, upper, lower))
        parts[r, owned:, :] = tail.astype(jnp.bfloat16)


def second_pass(stats, table, blocks):
    reduced, owned, d = table.shape
    g, n = stats.shape[1], stats.shape[3]
    k = owned * reduced
    return pl.pallas_call(
        second_kernel,
        in_specs=[pl.BlockSpec(memory_space=pltpu.VMEM)] * 5,
        out_specs=[pl.BlockSpec(memory_space=pltpu.VMEM)] * 2,
        out_shape=[
            jax.ShapeDtypeStruct((reduced, owned + 16, d), jnp.bfloat16),
            jax.ShapeDtypeStruct((1, n), jnp.float32),
        ],
        scratch_shapes=[
            pltpu.VMEM((g, n), jnp.float32),
            pltpu.VMEM((k, d), jnp.float32),
            pltpu.VMEM((k, 128), jnp.float32),
        ],
        compiler_params=pltpu.CompilerParams(vmem_limit_bytes=24 * MIB),
        cost_estimate=pl.CostEstimate(
            flops=4 * g * n * k * d, bytes_accessed=4 * k * d, transcendentals=g * n * k
        ),
        name="second_pass",
    )(stats, table.reshape(k, d), *blocks)


def last_kernel(parts, table, updated):
    owned = updated.shape[0]
    own = table[lax.axis_index(REDUCE)]
    sums = own.astype(jnp.float32)
    masses = jnp.ones((owned, owned), jnp.float32)
    for r in range(parts.shape[0]):
        tail = parts[r, owned:, :].astype(jnp.float32)
        mass = tail[1:2, :owned] + tail[1:2, owned:] + tail[2:3, :owned]
        mass = jnp.broadcast_to(mass, (owned, owned)).T
        code = parts[r, :owned, :].astype(jnp.float32)
        size = (jnp.log2(jnp.abs(code)) + FLOOR) * (tail[0:1, :] / SPAN)
        mean = jnp.where(code < 0.0, -size, size)
        weight = 1.0 + mass
        sums = sums + mean * jnp.concatenate([weight, weight], axis=1)
        masses = masses + mass
    updated[...] = sums / jnp.concatenate([masses, masses], axis=1)


def last_pass(parts, table):
    reduced, owned, d = table.shape
    return pl.pallas_call(
        last_kernel,
        in_specs=[pl.BlockSpec(memory_space=pltpu.VMEM)] * 2,
        out_specs=pl.BlockSpec(memory_space=pltpu.VMEM),
        out_shape=jax.ShapeDtypeStruct((owned, d), jnp.float32),
        compiler_params=pltpu.CompilerParams(vmem_limit_bytes=16 * MIB),
        name="last_pass",
    )(parts, table)


def moved(array, hops):
    low, cores, high = (lax.axis_size(a) for a in RING)
    ring = low * high

    def place(y, core):
        return ((y % low) * cores + core) * high + y // low

    pairs = [
        (place(y, core), place((y + hops[core]) % ring, core))
        for y in range(ring)
        for core in range(cores)
    ]
    return lax.ppermute(array, RING, pairs)


def body(points, centroids):
    n, d = points.shape
    cen = lax.axis_size(CEN)
    gathered = lax.axis_size(GATHER)
    reduced = lax.axis_size(REDUCE)
    owned = centroids.shape[0] // (gathered * reduced)

    far = moved(points, (2, -2))
    near = lax.all_gather(points, "co")
    side = moved(near, (1, -1))
    stats = first_pass(points, centroids, cen * gathered)
    far, side, _ = lax.optimization_barrier((far, side, stats))
    sides = lax.all_gather(side, "co")
    far = lax.all_gather(far, "co")
    every = lax.all_to_all(stats, (*CEN, *GATHER), 0, 0, tiled=True)
    every = every.reshape(cen, gathered, 2, n)
    sizes = [lax.axis_size(a) for a in AXES]
    at = (lax.axis_index("yl"), 0, lax.axis_index("co"), 0, 0)
    table = lax.dynamic_slice(
        centroids.reshape(*sizes, owned, d), at, (1, reduced, 1, owned, d)
    )
    table = lax.optimization_barrier(table.reshape(reduced, owned, d))
    parts, log_norm = second_pass(every, table, (near, sides, far))
    parts = lax.all_to_all(parts, REDUCE, 0, 0, tiled=True)
    return last_pass(parts, table), log_norm[0]


def solution(mesh):
    torus = Mesh(mesh.devices.reshape(4, 8, 2, 4, 2), (*AXES, *CEN))
    in_specs = (P(AXES, None), P(CEN, None))
    out_specs = (P((*CEN, *AXES), None), P(AXES))
    return jax.shard_map(body, mesh=torus, in_specs=in_specs, out_specs=out_specs, check_vma=False)
```

```python
import jax
import jax.numpy as jnp
from jax import lax
from jax.experimental import pallas as pl
from jax.experimental.pallas import tpu as pltpu
from jax.sharding import Mesh
from jax.sharding import PartitionSpec as P

AXES = ("yl", "z", "co")
CEN = ("x", "yh")
GATHER = ("yl", "co")
REDUCE = "z"
RING = ("yl", "co", "yh")
MIB = 1 << 20
CHUNK = 2048
inv_temp = 0.0625
SPAN, FLOOR = 240.0, 120.0


def squares(table):
    wide = table.astype(jnp.float32)
    return jnp.sum(wide * wide, axis=1, keepdims=True) * inv_temp


def columns(rows):
    return (rows * jnp.bfloat16(2.0 * inv_temp)).T


def products(table, columns):
    return jnp.dot(table, columns, preferred_element_type=jnp.float32)


def first_kernel(centroids, points, stats, reduced, table, rows, turned, arrived, ready):
    chunks = table.shape[0] // CHUNK

    def copy(i):
        here = pl.ds(i * CHUNK, CHUNK)
        return pltpu.make_async_copy(centroids.at[here], table.at[here], arrived.at[i])

    own = pltpu.make_async_copy(points, rows, ready)
    own.start()
    for i in range(chunks):
        copy(i).start()
    own.wait()
    turned[...] = columns(rows[...])

    def step(i, carry):
        peak, total = carry
        copy(i).wait()
        block = table[pl.ds(pl.multiple_of(i * CHUNK, CHUNK), CHUNK), :]
        logits = products(block, turned[...]) - squares(block)
        top = jnp.maximum(peak, jnp.max(logits, axis=0, keepdims=True))
        total = total * jnp.exp(peak - top) + jnp.sum(jnp.exp(logits - top), axis=0, keepdims=True)
        return top, total

    n = rows.shape[0]
    start = (jnp.full((1, n), -jnp.inf, jnp.float32), jnp.zeros((1, n), jnp.float32))
    peak, total = lax.fori_loop(0, chunks, step, start)
    both = jnp.concatenate([peak, total], axis=0)
    for i in range(stats.shape[0]):
        stats[i] = both
    yl, co = (lax.axis_index(a) for a in GATHER)
    count, owned, _ = reduced.shape
    for z in range(count):
        at = ((yl * count + z) * lax.axis_size("co") + co) * owned
        reduced[z] = table[pl.ds(pl.multiple_of(at, owned), owned), :]


def first_pass(points, centroids, receivers, reduced, owned):
    n, d = points.shape
    k = centroids.shape[0]
    return pl.pallas_call(
        first_kernel,
        in_specs=[pl.BlockSpec(memory_space=pltpu.HBM)] * 2,
        out_specs=[pl.BlockSpec(memory_space=pltpu.VMEM)] * 2,
        out_shape=[
            jax.ShapeDtypeStruct((receivers, 2, n), jnp.float32),
            jax.ShapeDtypeStruct((reduced, owned, d), centroids.dtype),
        ],
        scratch_shapes=[
            pltpu.VMEM((k, d), centroids.dtype),
            pltpu.VMEM((n, d), points.dtype),
            pltpu.VMEM((d, n), points.dtype),
            pltpu.SemaphoreType.DMA((k // CHUNK,)),
            pltpu.SemaphoreType.DMA,
        ],
        compiler_params=pltpu.CompilerParams(vmem_limit_bytes=24 * MIB),
        cost_estimate=pl.CostEstimate(
            flops=2 * n * k * d, bytes_accessed=2 * k * d, transcendentals=n * k
        ),
        name="first_pass",
    )(*(pltpu.with_memory_space_constraint(a, pltpu.HBM) for a in (centroids, points)))


def second_kernel(stats, table, near, sides, far, parts, own_norm, log_norms, sums, masses):
    yl, co = (lax.axis_index(a) for a in GATHER)

    cen = stats.shape[0]
    peak = stats[0, :, 0, :]
    for c in range(1, cen):
        peak = jnp.maximum(peak, stats[c, :, 0, :])
    total = stats[0, :, 1, :] * jnp.exp(stats[0, :, 0, :] - peak)
    for c in range(1, cen):
        total = total + stats[c, :, 1, :] * jnp.exp(stats[c, :, 0, :] - peak)
    log_norms[...] = peak + jnp.log(total)
    own_norm[...] = log_norms[pl.ds(yl * 2 + co, 1), :]

    norms = squares(table[...])
    pairs = ((near, 0), (sides.at[0], 3), (sides.at[1], 1), (far, 2))
    for at, (rows, off) in enumerate(pairs):
        for c in range(2):
            shift = log_norms[pl.ds(lax.rem(yl + off, 4) * 2 + c, 1), :]
            logits = products(table[...], columns(rows[c])) - norms
            shares = jnp.exp(logits - shift).astype(jnp.bfloat16)
            product = lax.dot_general(
                shares, rows[c], (((1,), (0,)), ((), ())), preferred_element_type=jnp.float32
            )
            wide = shares.astype(jnp.float32)
            mass = wide[:, :128] + wide[:, 128:]
            if at == 0 and c == 0:
                sums[...] = product
                masses[...] = mass
            else:
                sums[...] += product
                masses[...] += mass

    owned, d = parts.shape[1] - 16, parts.shape[2]
    line = lax.broadcasted_iota(jnp.int32, (16, d), 0)
    for r in range(parts.shape[0]):
        here = slice(r * owned, (r + 1) * owned)
        mass = masses[here, :]
        mean = sums[here, :] / (1.0 + jnp.sum(mass, axis=1, keepdims=True))
        size = jnp.abs(mean)
        scale = jnp.maximum(jnp.max(size, axis=0, keepdims=True) * 1.01, 1e-30)
        scale = scale.astype(jnp.bfloat16).astype(jnp.float32)
        code = jnp.exp2(size * (SPAN / scale) - FLOOR)
        parts[r, :owned, :] = jnp.where(mean < 0.0, -code, code).astype(jnp.bfloat16)
        mass = jnp.sum(mass.T, axis=0, keepdims=True)
        high = mass.astype(jnp.bfloat16).astype(jnp.float32)
        mid = (mass - high).astype(jnp.bfloat16).astype(jnp.float32)
        low = mass - high - mid
        upper = jnp.concatenate([high, mid], axis=1)
        lower = jnp.concatenate([low, jnp.zeros_like(low)], axis=1)
        tail = jnp.where(line == 0, scale, jnp.where(line == 1, upper, lower))
        parts[r, owned:, :] = tail.astype(jnp.bfloat16)


def second_pass(stats, table, blocks):
    reduced, owned, d = table.shape
    g, n = stats.shape[1], stats.shape[3]
    k = owned * reduced
    return pl.pallas_call(
        second_kernel,
        in_specs=[pl.BlockSpec(memory_space=pltpu.VMEM)] * 5,
        out_specs=[pl.BlockSpec(memory_space=pltpu.VMEM)] * 2,
        out_shape=[
            jax.ShapeDtypeStruct((reduced, owned + 16, d), jnp.bfloat16),
            jax.ShapeDtypeStruct((1, n), jnp.float32),
        ],
        scratch_shapes=[
            pltpu.VMEM((g, n), jnp.float32),
            pltpu.VMEM((k, d), jnp.float32),
            pltpu.VMEM((k, 128), jnp.float32),
        ],
        compiler_params=pltpu.CompilerParams(vmem_limit_bytes=24 * MIB),
        cost_estimate=pl.CostEstimate(
            flops=4 * g * n * k * d, bytes_accessed=4 * k * d, transcendentals=g * n * k
        ),
        name="second_pass",
    )(stats, table.reshape(k, d), *blocks)


def last_kernel(parts, table, updated):
    owned = updated.shape[0]
    own = table[lax.axis_index(REDUCE)]
    sums = own.astype(jnp.float32)
    masses = jnp.ones((owned, owned), jnp.float32)
    for r in range(parts.shape[0]):
        tail = parts[r, owned:, :].astype(jnp.float32)
        mass = tail[1:2, :owned] + tail[1:2, owned:] + tail[2:3, :owned]
        mass = jnp.broadcast_to(mass, (owned, owned)).T
        code = parts[r, :owned, :].astype(jnp.float32)
        size = (jnp.log2(jnp.abs(code)) + FLOOR) * (tail[0:1, :] / SPAN)
        mean = jnp.where(code < 0.0, -size, size)
        weight = 1.0 + mass
        sums = sums + mean * jnp.concatenate([weight, weight], axis=1)
        masses = masses + mass
    updated[...] = sums / jnp.concatenate([masses, masses], axis=1)


def last_pass(parts, table):
    reduced, owned, d = table.shape
    return pl.pallas_call(
        last_kernel,
        in_specs=[pl.BlockSpec(memory_space=pltpu.VMEM)] * 2,
        out_specs=pl.BlockSpec(memory_space=pltpu.VMEM),
        out_shape=jax.ShapeDtypeStruct((owned, d), jnp.float32),
        compiler_params=pltpu.CompilerParams(vmem_limit_bytes=16 * MIB),
        name="last_pass",
    )(parts, table)


def moved(array, hops):
    low, cores, high = (lax.axis_size(a) for a in RING)
    ring = low * high

    def place(y, core):
        return ((y % low) * cores + core) * high + y // low

    pairs = [
        (place(y, core), place((y + hops[core]) % ring, core))
        for y in range(ring)
        for core in range(cores)
    ]
    return lax.ppermute(array, RING, pairs)


def body(points, centroids):
    n, d = points.shape
    cen = lax.axis_size(CEN)
    gathered = lax.axis_size(GATHER)
    reduced = lax.axis_size(REDUCE)
    owned = centroids.shape[0] // (gathered * reduced)

    near = lax.all_gather(points, "co")
    side, far = moved(near, (1, -1)), moved(near, (2, -2))
    stats, table = first_pass(points, centroids, cen * gathered, reduced, owned)
    side, _ = lax.optimization_barrier((side, stats))
    sides = lax.all_gather(side, "co")
    every = lax.all_to_all(stats, (*CEN, *GATHER), 0, 0, tiled=True)
    every = every.reshape(cen, gathered, 2, n)
    parts, log_norm = second_pass(every, table, (near, sides, far))
    parts = lax.all_to_all(parts, REDUCE, 0, 0, tiled=True)
    return last_pass(parts, table), log_norm[0]


def solution(mesh):
    torus = Mesh(mesh.devices.reshape(4, 8, 2, 4, 2), (*AXES, *CEN))
    in_specs = (P(AXES, None), P(CEN, None))
    out_specs = (P((*CEN, *AXES), None), P(AXES))
    return jax.shard_map(body, mesh=torus, in_specs=in_specs, out_specs=out_specs, check_vma=False)
```

```python
import jax
import jax.numpy as jnp
from jax import lax
from jax.experimental import pallas as pl
from jax.experimental.pallas import tpu as pltpu
from jax.sharding import Mesh
from jax.sharding import PartitionSpec as P

AXES = ("yl", "z", "co")
CEN = ("x", "yh")
GATHER = ("yl", "co")
REDUCE = "z"
RING = ("yl", "co", "yh")
MIB = 1 << 20
CHUNK = 2048
inv_temp = 0.0625
SPAN, FLOOR = 240.0, 120.0


def squares(table):
    wide = table.astype(jnp.float32)
    return jnp.sum(wide * wide, axis=1, keepdims=True) * inv_temp


def columns(rows):
    return (rows * jnp.bfloat16(2.0 * inv_temp)).T


def products(table, columns):
    return jnp.dot(table, columns, preferred_element_type=jnp.float32)


def first_kernel(centroids, points, stats, reduced, table, rows, turned, arrived, ready):
    chunks = table.shape[0] // CHUNK

    def copy(i):
        here = pl.ds(i * CHUNK, CHUNK)
        return pltpu.make_async_copy(centroids.at[here], table.at[here], arrived.at[i])

    own = pltpu.make_async_copy(points, rows, ready)
    own.start()
    for i in range(chunks):
        copy(i).start()
    own.wait()
    turned[...] = columns(rows[...])

    def step(i, carry):
        peak, total = carry
        copy(i).wait()
        block = table[pl.ds(pl.multiple_of(i * CHUNK, CHUNK), CHUNK), :]
        logits = products(block, turned[...]) - squares(block)
        top = jnp.maximum(peak, jnp.max(logits, axis=0, keepdims=True))
        total = total * jnp.exp(peak - top) + jnp.sum(jnp.exp(logits - top), axis=0, keepdims=True)
        return top, total

    n = rows.shape[0]
    start = (jnp.full((1, n), -jnp.inf, jnp.float32), jnp.zeros((1, n), jnp.float32))
    peak, total = lax.fori_loop(0, chunks, step, start)
    both = jnp.concatenate([peak, total], axis=0)
    for i in range(stats.shape[0]):
        stats[i] = both
    yl, co = (lax.axis_index(a) for a in GATHER)
    count, owned, _ = reduced.shape
    for z in range(count):
        at = ((yl * count + z) * lax.axis_size("co") + co) * owned
        reduced[z] = table[pl.ds(pl.multiple_of(at, owned), owned), :]


def first_pass(points, centroids, receivers, reduced, owned):
    n, d = points.shape
    k = centroids.shape[0]
    return pl.pallas_call(
        first_kernel,
        in_specs=[pl.BlockSpec(memory_space=pltpu.HBM)] * 2,
        out_specs=[pl.BlockSpec(memory_space=pltpu.VMEM)] * 2,
        out_shape=[
            jax.ShapeDtypeStruct((receivers, 2, n), jnp.float32),
            jax.ShapeDtypeStruct((reduced, owned, d), centroids.dtype),
        ],
        scratch_shapes=[
            pltpu.VMEM((k, d), centroids.dtype),
            pltpu.VMEM((n, d), points.dtype),
            pltpu.VMEM((d, n), points.dtype),
            pltpu.SemaphoreType.DMA((k // CHUNK,)),
            pltpu.SemaphoreType.DMA,
        ],
        compiler_params=pltpu.CompilerParams(vmem_limit_bytes=24 * MIB),
        cost_estimate=pl.CostEstimate(
            flops=2 * n * k * d, bytes_accessed=2 * k * d, transcendentals=n * k
        ),
        name="first_pass",
    )(*(pltpu.with_memory_space_constraint(a, pltpu.HBM) for a in (centroids, points)))


def second_kernel(stats, table, near, sides, far, parts, own_norm, log_norms, sums, masses):
    yl, co = (lax.axis_index(a) for a in GATHER)

    cen = stats.shape[0]
    peak = stats[0, :, 0, :]
    for c in range(1, cen):
        peak = jnp.maximum(peak, stats[c, :, 0, :])
    total = stats[0, :, 1, :] * jnp.exp(stats[0, :, 0, :] - peak)
    for c in range(1, cen):
        total = total + stats[c, :, 1, :] * jnp.exp(stats[c, :, 0, :] - peak)
    log_norms[...] = peak + jnp.log(total)
    own_norm[...] = log_norms[pl.ds(yl * 2 + co, 1), :]

    norms = squares(table[...])
    cores, n, d = near.shape
    pairs = ((near, 0), (sides.at[0], 3), (sides.at[1], 1), (far, 2))
    for at, (rows, off) in enumerate(pairs):
        chip = lax.rem(yl + off, 4) * cores
        shift = [log_norms[pl.ds(chip + c, 1), :] for c in range(cores)]
        pair = rows[...].reshape(cores * n, d)
        logits = products(table[...], columns(pair)) - norms
        shares = jnp.exp(logits - jnp.concatenate(shift, axis=1)).astype(jnp.bfloat16)
        product = jnp.dot(shares, pair, preferred_element_type=jnp.float32)
        wide = shares.astype(jnp.float32)
        mass = sum(wide[:, i : i + 128] for i in range(0, cores * n, 128))
        if at == 0:
            sums[...] = product
            masses[...] = mass
        else:
            sums[...] += product
            masses[...] += mass

    owned = sums.shape[0] // parts.shape[0]
    line = lax.broadcasted_iota(jnp.int32, (16, 128), 0)
    for r in range(parts.shape[0]):
        here = slice(r * owned, (r + 1) * owned)
        mass = masses[here, :]
        mean = sums[here, :] / (1.0 + jnp.sum(mass, axis=1, keepdims=True))
        size = jnp.abs(mean)
        scale = jnp.maximum(jnp.max(size, axis=0, keepdims=True) * 1.01, 1e-30)
        scale = scale.astype(jnp.bfloat16).astype(jnp.float32)
        code = jnp.exp2(size * (SPAN / scale) - FLOOR)
        code = jnp.where(mean < 0.0, -code, code).astype(jnp.bfloat16)
        parts[r, :owned, :] = code[:, :128]
        parts[r, owned : 2 * owned, :] = code[:, 128:]
        mass = jnp.sum(mass.T, axis=0, keepdims=True)
        high = mass.astype(jnp.bfloat16).astype(jnp.float32)
        mid = (mass - high).astype(jnp.bfloat16).astype(jnp.float32)
        tail = mass - high - mid
        for at, row in enumerate((scale[:, :128], scale[:, 128:], high, mid)):
            tail = jnp.where(line == at, row, tail)
        parts[r, 2 * owned :, :] = tail.astype(jnp.bfloat16)


def second_pass(stats, table, blocks):
    reduced, owned, d = table.shape
    g, n = stats.shape[1], stats.shape[3]
    k = owned * reduced
    return pl.pallas_call(
        second_kernel,
        in_specs=[pl.BlockSpec(memory_space=pltpu.VMEM)] * 5,
        out_specs=[pl.BlockSpec(memory_space=pltpu.VMEM)] * 2,
        out_shape=[
            jax.ShapeDtypeStruct((reduced, 2 * owned + 16, d // 2), jnp.bfloat16),
            jax.ShapeDtypeStruct((1, n), jnp.float32),
        ],
        scratch_shapes=[
            pltpu.VMEM((g, n), jnp.float32),
            pltpu.VMEM((k, d), jnp.float32),
            pltpu.VMEM((k, 128), jnp.float32),
        ],
        compiler_params=pltpu.CompilerParams(vmem_limit_bytes=24 * MIB),
        cost_estimate=pl.CostEstimate(
            flops=4 * g * n * k * d, bytes_accessed=4 * k * d, transcendentals=g * n * k
        ),
        name="second_pass",
    )(stats, table.reshape(k, d), *blocks)


def last_kernel(parts, table, updated):
    owned = updated.shape[0]
    own = table[lax.axis_index(REDUCE)]
    sums = own.astype(jnp.float32)
    masses = jnp.ones((owned, owned), jnp.float32)
    for r in range(parts.shape[0]):
        tail = parts[r, 2 * owned :, :].astype(jnp.float32)
        mass = jnp.broadcast_to(tail[2:3] + tail[3:4] + tail[4:5], (owned, owned)).T
        means = []
        for half in range(2):
            code = parts[r, half * owned : (half + 1) * owned, :].astype(jnp.float32)
            size = (jnp.log2(jnp.abs(code)) + FLOOR) * (tail[half : half + 1] / SPAN)
            means.append(jnp.where(code < 0.0, -size, size) * (1.0 + mass))
        sums = sums + jnp.concatenate(means, axis=1)
        masses = masses + mass
    updated[...] = sums / jnp.concatenate([masses, masses], axis=1)


def last_pass(parts, table):
    reduced, owned, d = table.shape
    return pl.pallas_call(
        last_kernel,
        in_specs=[pl.BlockSpec(memory_space=pltpu.VMEM)] * 2,
        out_specs=pl.BlockSpec(memory_space=pltpu.VMEM),
        out_shape=jax.ShapeDtypeStruct((owned, d), jnp.float32),
        compiler_params=pltpu.CompilerParams(vmem_limit_bytes=16 * MIB),
        name="last_pass",
    )(parts, table)


def moved(array, hops):
    low, cores, high = (lax.axis_size(a) for a in RING)
    ring = low * high

    def place(y, core):
        return ((y % low) * cores + core) * high + y // low

    pairs = [
        (place(y, core), place((y + hops[core]) % ring, core))
        for y in range(ring)
        for core in range(cores)
    ]
    return lax.ppermute(array, RING, pairs)


def body(points, centroids):
    n, d = points.shape
    cen = lax.axis_size(CEN)
    gathered = lax.axis_size(GATHER)
    reduced = lax.axis_size(REDUCE)
    owned = centroids.shape[0] // (gathered * reduced)

    near = lax.all_gather(points, "co")
    side, far = moved(near, (1, -1)), moved(near, (2, -2))
    stats, table = first_pass(points, centroids, cen * gathered, reduced, owned)
    side, _ = lax.optimization_barrier((side, stats))
    sides = lax.all_gather(side, "co")
    every = lax.all_to_all(stats, (*CEN, *GATHER), 0, 0, tiled=True)
    every = every.reshape(cen, gathered, 2, n)
    parts, log_norm = second_pass(every, table, (near, sides, far))
    parts = lax.all_to_all(parts, REDUCE, 0, 0, tiled=True)
    return last_pass(parts, table), log_norm[0]


def solution(mesh):
    torus = Mesh(mesh.devices.reshape(4, 8, 2, 4, 2), (*AXES, *CEN))
    in_specs = (P(AXES, None), P(CEN, None))
    out_specs = (P((*CEN, *AXES), None), P(AXES))
    return jax.shard_map(body, mesh=torus, in_specs=in_specs, out_specs=out_specs, check_vma=False)
```

```python
import jax
import jax.numpy as jnp
from jax import lax
from jax.experimental import pallas as pl
from jax.experimental.pallas import tpu as pltpu
from jax.sharding import Mesh
from jax.sharding import PartitionSpec as P

AXES = ("ya", "yb", "za", "zb", "co")
CEN = ("x", "yh")
SQUARE = ("yb", "zb")
GATHER = ("yb", "zb", "co")
REDUCE = ("ya", "za")
MIB = 1 << 20
CHUNK = 2048
inv_temp = 0.0625
SPAN, FLOOR = 240.0, 120.0


def squares(table):
    wide = table.astype(jnp.float32)
    return jnp.sum(wide * wide, axis=1, keepdims=True) * inv_temp


def columns(rows):
    return (rows * jnp.bfloat16(2.0 * inv_temp)).T


def products(table, columns):
    return jnp.dot(table, columns, preferred_element_type=jnp.float32)


def first_kernel(centroids, points, stats, reduced, table, rows, turned, arrived, ready):
    chunks = table.shape[0] // CHUNK

    def copy(i):
        here = pl.ds(i * CHUNK, CHUNK)
        return pltpu.make_async_copy(centroids.at[here], table.at[here], arrived.at[i])

    own = pltpu.make_async_copy(points, rows, ready)
    own.start()
    for i in range(chunks):
        copy(i).start()
    own.wait()
    turned[...] = columns(rows[...])

    def step(i, carry):
        peak, total = carry
        copy(i).wait()
        block = table[pl.ds(pl.multiple_of(i * CHUNK, CHUNK), CHUNK), :]
        logits = products(block, turned[...]) - squares(block)
        top = jnp.maximum(peak, jnp.max(logits, axis=0, keepdims=True))
        total = total * jnp.exp(peak - top) + jnp.sum(jnp.exp(logits - top), axis=0, keepdims=True)
        return top, total

    n = rows.shape[0]
    start = (jnp.full((1, n), -jnp.inf, jnp.float32), jnp.zeros((1, n), jnp.float32))
    peak, total = lax.fori_loop(0, chunks, step, start)
    both = jnp.concatenate([peak, total], axis=0)
    for i in range(stats.shape[0]):
        stats[i] = both
    owned = reduced.shape[1]
    place = {a: lax.axis_index(a) for a in AXES}
    for r in range(reduced.shape[0]):
        place["ya"], place["za"] = divmod(r, lax.axis_size("za"))
        at = 0
        for a in AXES:
            at = at * lax.axis_size(a) + place[a]
        reduced[r] = table[pl.ds(pl.multiple_of(at * owned, owned), owned), :]


def first_pass(points, centroids, receivers, reduced, owned):
    n, d = points.shape
    k = centroids.shape[0]
    return pl.pallas_call(
        first_kernel,
        in_specs=[pl.BlockSpec(memory_space=pltpu.HBM)] * 2,
        out_specs=[pl.BlockSpec(memory_space=pltpu.VMEM)] * 2,
        out_shape=[
            jax.ShapeDtypeStruct((receivers, 2, n), jnp.float32),
            jax.ShapeDtypeStruct((reduced, owned, d), centroids.dtype),
        ],
        scratch_shapes=[
            pltpu.VMEM((k, d), centroids.dtype),
            pltpu.VMEM((n, d), points.dtype),
            pltpu.VMEM((d, n), points.dtype),
            pltpu.SemaphoreType.DMA((k // CHUNK,)),
            pltpu.SemaphoreType.DMA,
        ],
        compiler_params=pltpu.CompilerParams(vmem_limit_bytes=24 * MIB),
        cost_estimate=pl.CostEstimate(
            flops=2 * n * k * d, bytes_accessed=2 * k * d, transcendentals=n * k
        ),
        name="first_pass",
    )(*(pltpu.with_memory_space_constraint(a, pltpu.HBM) for a in (centroids, points)))


def second_kernel(stats, table, here, there, parts, own_norm, log_norms, sums, masses):
    co = lax.axis_index("co")

    cen = stats.shape[0]
    peak = stats[0, :, 0, :]
    for c in range(1, cen):
        peak = jnp.maximum(peak, stats[c, :, 0, :])
    total = stats[0, :, 1, :] * jnp.exp(stats[0, :, 0, :] - peak)
    for c in range(1, cen):
        total = total + stats[c, :, 1, :] * jnp.exp(stats[c, :, 0, :] - peak)
    log_norms[...] = peak + jnp.log(total)
    own_norm[...] = log_norms[pl.ds(lax.axis_index(SQUARE) * 2 + co, 1), :]

    norms = squares(table[...])
    chips, n, d = here.shape
    pairs = [(rows, core, at) for rows, core in ((here, co), (there, 1 - co)) for at in (0, 2)]
    for rows, core, at in pairs:
        shift = [log_norms[pl.ds((at + i) * 2 + core, 1), :] for i in range(2)]
        pair = rows[at : at + 2].reshape(2 * n, d)
        logits = products(table[...], columns(pair)) - norms
        shares = jnp.exp(logits - jnp.concatenate(shift, axis=1)).astype(jnp.bfloat16)
        product = jnp.dot(shares, pair, preferred_element_type=jnp.float32)
        wide = shares.astype(jnp.float32)
        mass = sum(wide[:, i : i + 128] for i in range(0, 2 * n, 128))
        if rows is here and at == 0:
            sums[...] = product
            masses[...] = mass
        else:
            sums[...] += product
            masses[...] += mass

    owned = sums.shape[0] // parts.shape[0]
    line = lax.broadcasted_iota(jnp.int32, (16, 128), 0)
    for r in range(parts.shape[0]):
        here = slice(r * owned, (r + 1) * owned)
        mass = masses[here, :]
        mean = sums[here, :] / (1.0 + jnp.sum(mass, axis=1, keepdims=True))
        size = jnp.abs(mean)
        scale = jnp.maximum(jnp.max(size, axis=0, keepdims=True) * 1.01, 1e-30)
        scale = scale.astype(jnp.bfloat16).astype(jnp.float32)
        code = jnp.exp2(size * (SPAN / scale) - FLOOR)
        code = jnp.where(mean < 0.0, -code, code).astype(jnp.bfloat16)
        parts[r, :owned, :] = code[:, :128]
        parts[r, owned : 2 * owned, :] = code[:, 128:]
        mass = jnp.sum(mass.T, axis=0, keepdims=True)
        high = mass.astype(jnp.bfloat16).astype(jnp.float32)
        mid = (mass - high).astype(jnp.bfloat16).astype(jnp.float32)
        tail = mass - high - mid
        for at, row in enumerate((scale[:, :128], scale[:, 128:], high, mid)):
            tail = jnp.where(line == at, row, tail)
        parts[r, 2 * owned :, :] = tail.astype(jnp.bfloat16)


def second_pass(stats, table, blocks):
    reduced, owned, d = table.shape
    g, n = stats.shape[1], stats.shape[3]
    k = owned * reduced
    return pl.pallas_call(
        second_kernel,
        in_specs=[pl.BlockSpec(memory_space=pltpu.VMEM)] * 4,
        out_specs=[pl.BlockSpec(memory_space=pltpu.VMEM)] * 2,
        out_shape=[
            jax.ShapeDtypeStruct((reduced, 2 * owned + 16, d // 2), jnp.bfloat16),
            jax.ShapeDtypeStruct((1, n), jnp.float32),
        ],
        scratch_shapes=[
            pltpu.VMEM((g, n), jnp.float32),
            pltpu.VMEM((k, d), jnp.float32),
            pltpu.VMEM((k, 128), jnp.float32),
        ],
        compiler_params=pltpu.CompilerParams(vmem_limit_bytes=24 * MIB),
        cost_estimate=pl.CostEstimate(
            flops=4 * g * n * k * d, bytes_accessed=4 * k * d, transcendentals=g * n * k
        ),
        name="second_pass",
    )(stats, table.reshape(k, d), *blocks)


def last_kernel(parts, table, updated):
    owned = updated.shape[0]
    own = table[lax.axis_index(REDUCE)]
    sums = own.astype(jnp.float32)
    masses = jnp.ones((owned, owned), jnp.float32)
    for r in range(parts.shape[0]):
        tail = parts[r, 2 * owned :, :].astype(jnp.float32)
        mass = jnp.broadcast_to(tail[2:3] + tail[3:4] + tail[4:5], (owned, owned)).T
        means = []
        for half in range(2):
            code = parts[r, half * owned : (half + 1) * owned, :].astype(jnp.float32)
            size = (jnp.log2(jnp.abs(code)) + FLOOR) * (tail[half : half + 1] / SPAN)
            means.append(jnp.where(code < 0.0, -size, size) * (1.0 + mass))
        sums = sums + jnp.concatenate(means, axis=1)
        masses = masses + mass
    updated[...] = sums / jnp.concatenate([masses, masses], axis=1)


def last_pass(parts, table):
    reduced, owned, d = table.shape
    return pl.pallas_call(
        last_kernel,
        in_specs=[pl.BlockSpec(memory_space=pltpu.VMEM)] * 2,
        out_specs=pl.BlockSpec(memory_space=pltpu.VMEM),
        out_shape=jax.ShapeDtypeStruct((owned, d), jnp.float32),
        compiler_params=pltpu.CompilerParams(vmem_limit_bytes=16 * MIB),
        name="last_pass",
    )(parts, table)


def body(points, centroids):
    n, d = points.shape
    cen = lax.axis_size(CEN)
    gathered = lax.axis_size(GATHER)
    reduced = lax.axis_size(REDUCE)
    owned = centroids.shape[0] // (gathered * reduced)

    copies = jnp.broadcast_to(points, (lax.axis_size(SQUARE), n, d))
    here = lax.all_to_all(copies, SQUARE, 0, 0, tiled=True)
    stats, table = first_pass(points, centroids, cen * gathered, reduced, owned)
    after, _ = lax.optimization_barrier((here, stats))
    there = lax.ppermute(after, "co", [(0, 1), (1, 0)])
    every = lax.all_to_all(stats, (*CEN, *GATHER), 0, 0, tiled=True)
    every = every.reshape(cen, gathered, 2, n)
    parts, log_norm = second_pass(every, table, (here, there))
    parts = lax.all_to_all(parts, REDUCE, 0, 0, tiled=True)
    return last_pass(parts, table), log_norm[0]


def solution(mesh):
    torus = Mesh(mesh.devices.reshape(2, 2, 4, 2, 2, 4, 2), (*AXES, *CEN))
    in_specs = (P(AXES, None), P(CEN, None))
    out_specs = (P((*CEN, *AXES), None), P(AXES))
    return jax.shard_map(body, mesh=torus, in_specs=in_specs, out_specs=out_specs, check_vma=False)
```

```python
import jax
import jax.numpy as jnp
from jax import lax
from jax.experimental import pallas as pl
from jax.experimental.pallas import tpu as pltpu
from jax.sharding import Mesh
from jax.sharding import PartitionSpec as P

AXES = ("yl", "z", "co")
CEN = ("x", "yh")
GATHER = ("yl", "co")
REDUCE = "z"
RING = ("yl", "co", "yh")
MIB = 1 << 20
CHUNK = 2048
inv_temp = 0.0625
SPAN, FLOOR = 240.0, 120.0


def squares(table):
    wide = table.astype(jnp.float32)
    return jnp.sum(wide * wide, axis=1, keepdims=True) * inv_temp


def columns(rows):
    return (rows * jnp.bfloat16(2.0 * inv_temp)).T


def products(table, columns):
    return jnp.dot(table, columns, preferred_element_type=jnp.float32)


def first_kernel(centroids, points, stats, reduced, table, rows, turned, arrived, ready):
    pieces = (slice(0, CHUNK), slice(CHUNK, table.shape[0]))
    own = pltpu.make_async_copy(points, rows, ready)
    copies = [
        pltpu.make_async_copy(centroids.at[piece], table.at[piece], arrived.at[i])
        for i, piece in enumerate(pieces)
    ]
    own.start()
    for copy in copies:
        copy.start()
    own.wait()
    turned[...] = columns(rows[...])

    found = []
    for copy, piece in zip(copies, pieces):
        copy.wait()
        block = table[piece, :]
        logits = products(block, turned[...]) - squares(block)
        top = jnp.max(logits, axis=0, keepdims=True)
        found.append((top, jnp.sum(jnp.exp(logits - top), axis=0, keepdims=True)))
    peak = jnp.maximum(found[0][0], found[1][0])
    total = sum(part * jnp.exp(top - peak) for top, part in found)
    both = jnp.concatenate([peak, total], axis=0)
    for i in range(stats.shape[0]):
        stats[i] = both
    yl, co = (lax.axis_index(a) for a in GATHER)
    count, owned, _ = reduced.shape
    for z in range(count):
        at = ((yl * count + z) * lax.axis_size("co") + co) * owned
        reduced[z] = table[pl.ds(pl.multiple_of(at, owned), owned), :]


def first_pass(points, centroids, receivers, reduced, owned):
    n, d = points.shape
    k = centroids.shape[0]
    return pl.pallas_call(
        first_kernel,
        in_specs=[pl.BlockSpec(memory_space=pltpu.HBM)] * 2,
        out_specs=[pl.BlockSpec(memory_space=pltpu.VMEM)] * 2,
        out_shape=[
            jax.ShapeDtypeStruct((receivers, 2, n), jnp.float32),
            jax.ShapeDtypeStruct((reduced, owned, d), centroids.dtype),
        ],
        scratch_shapes=[
            pltpu.VMEM((k, d), centroids.dtype),
            pltpu.VMEM((n, d), points.dtype),
            pltpu.VMEM((d, n), points.dtype),
            pltpu.SemaphoreType.DMA((2,)),
            pltpu.SemaphoreType.DMA,
        ],
        compiler_params=pltpu.CompilerParams(vmem_limit_bytes=32 * MIB),
        cost_estimate=pl.CostEstimate(
            flops=2 * n * k * d, bytes_accessed=2 * k * d, transcendentals=n * k
        ),
        name="first_pass",
    )(*(pltpu.with_memory_space_constraint(a, pltpu.HBM) for a in (centroids, points)))


def second_kernel(stats, table, near, sides, far, parts, own_norm, log_norms, sums, masses):
    yl, co = (lax.axis_index(a) for a in GATHER)

    cen = stats.shape[0]
    peak = stats[0, :, 0, :]
    for c in range(1, cen):
        peak = jnp.maximum(peak, stats[c, :, 0, :])
    total = stats[0, :, 1, :] * jnp.exp(stats[0, :, 0, :] - peak)
    for c in range(1, cen):
        total = total + stats[c, :, 1, :] * jnp.exp(stats[c, :, 0, :] - peak)
    log_norms[...] = peak + jnp.log(total)
    own_norm[...] = log_norms[pl.ds(yl * 2 + co, 1), :]

    norms = squares(table[...])
    cores, n, d = near.shape
    groups = ((near, (0,)), (sides, (3, 1)), (far, (2,)))
    for rows, offs in groups:
        chips = [lax.rem(yl + off, 4) * cores for off in offs]
        shift = [log_norms[pl.ds(chip + c, 1), :] for chip in chips for c in range(cores)]
        count = len(shift) * n
        points = rows[...].reshape(count, d)
        logits = products(table[...], columns(points)) - norms
        shares = jnp.exp(logits - jnp.concatenate(shift, axis=1)).astype(jnp.bfloat16)
        product = jnp.dot(shares, points, preferred_element_type=jnp.float32)
        wide = shares.astype(jnp.float32)
        mass = sum(wide[:, i : i + 128] for i in range(0, count, 128))
        if rows is near:
            sums[...] = product
            masses[...] = mass
        else:
            sums[...] += product
            masses[...] += mass

    owned = sums.shape[0] // parts.shape[0]
    line = lax.broadcasted_iota(jnp.int32, (16, 128), 0)
    for r in range(parts.shape[0]):
        here = slice(r * owned, (r + 1) * owned)
        mass = masses[here, :]
        mean = sums[here, :] / (1.0 + jnp.sum(mass, axis=1, keepdims=True))
        size = jnp.abs(mean)
        scale = jnp.maximum(jnp.max(size, axis=0, keepdims=True) * 1.01, 1e-30)
        scale = scale.astype(jnp.bfloat16).astype(jnp.float32)
        code = jnp.exp2(size * (SPAN / scale) - FLOOR)
        code = jnp.where(mean < 0.0, -code, code).astype(jnp.bfloat16)
        parts[r, :owned, :] = code[:, :128]
        parts[r, owned : 2 * owned, :] = code[:, 128:]
        mass = jnp.sum(mass.T, axis=0, keepdims=True)
        high = mass.astype(jnp.bfloat16).astype(jnp.float32)
        mid = (mass - high).astype(jnp.bfloat16).astype(jnp.float32)
        tail = mass - high - mid
        for at, row in enumerate((scale[:, :128], scale[:, 128:], high, mid)):
            tail = jnp.where(line == at, row, tail)
        parts[r, 2 * owned :, :] = tail.astype(jnp.bfloat16)


def second_pass(stats, table, blocks):
    reduced, owned, d = table.shape
    g, n = stats.shape[1], stats.shape[3]
    k = owned * reduced
    return pl.pallas_call(
        second_kernel,
        in_specs=[pl.BlockSpec(memory_space=pltpu.VMEM)] * 5,
        out_specs=[pl.BlockSpec(memory_space=pltpu.VMEM)] * 2,
        out_shape=[
            jax.ShapeDtypeStruct((reduced, 2 * owned + 16, d // 2), jnp.bfloat16),
            jax.ShapeDtypeStruct((1, n), jnp.float32),
        ],
        scratch_shapes=[
            pltpu.VMEM((g, n), jnp.float32),
            pltpu.VMEM((k, d), jnp.float32),
            pltpu.VMEM((k, 128), jnp.float32),
        ],
        compiler_params=pltpu.CompilerParams(vmem_limit_bytes=24 * MIB),
        cost_estimate=pl.CostEstimate(
            flops=4 * g * n * k * d, bytes_accessed=4 * k * d, transcendentals=g * n * k
        ),
        name="second_pass",
    )(stats, table.reshape(k, d), *blocks)


def last_kernel(parts, table, updated):
    owned = updated.shape[0]
    own = table[lax.axis_index(REDUCE)]
    sums = own.astype(jnp.float32)
    masses = jnp.ones((owned, owned), jnp.float32)
    for r in range(parts.shape[0]):
        tail = parts[r, 2 * owned :, :].astype(jnp.float32)
        mass = jnp.broadcast_to(tail[2:3] + tail[3:4] + tail[4:5], (owned, owned)).T
        means = []
        for half in range(2):
            code = parts[r, half * owned : (half + 1) * owned, :].astype(jnp.float32)
            size = (jnp.log2(jnp.abs(code)) + FLOOR) * (tail[half : half + 1] / SPAN)
            means.append(jnp.where(code < 0.0, -size, size) * (1.0 + mass))
        sums = sums + jnp.concatenate(means, axis=1)
        masses = masses + mass
    updated[...] = sums / jnp.concatenate([masses, masses], axis=1)


def last_pass(parts, table):
    reduced, owned, d = table.shape
    return pl.pallas_call(
        last_kernel,
        in_specs=[pl.BlockSpec(memory_space=pltpu.VMEM)] * 2,
        out_specs=pl.BlockSpec(memory_space=pltpu.VMEM),
        out_shape=jax.ShapeDtypeStruct((owned, d), jnp.float32),
        compiler_params=pltpu.CompilerParams(vmem_limit_bytes=16 * MIB),
        name="last_pass",
    )(parts, table)


def moved(array, hops):
    low, cores, high = (lax.axis_size(a) for a in RING)
    ring = low * high

    def place(y, core):
        return ((y % low) * cores + core) * high + y // low

    pairs = [
        (place(y, core), place((y + hops[core]) % ring, core))
        for y in range(ring)
        for core in range(cores)
    ]
    return lax.ppermute(array, RING, pairs)


def body(points, centroids):
    n, d = points.shape
    cen = lax.axis_size(CEN)
    gathered = lax.axis_size(GATHER)
    reduced = lax.axis_size(REDUCE)
    owned = centroids.shape[0] // (gathered * reduced)

    near = lax.all_gather(points, "co")
    side, far = moved(near, (1, -1)), moved(near, (2, -2))
    stats, table = first_pass(points, centroids, cen * gathered, reduced, owned)
    side, _ = lax.optimization_barrier((side, stats))
    sides = lax.all_gather(side, "co")
    every = lax.all_to_all(stats, (*CEN, *GATHER), 0, 0, tiled=True)
    every = every.reshape(cen, gathered, 2, n)
    parts, log_norm = second_pass(every, table, (near, sides, far))
    parts = lax.all_to_all(parts, REDUCE, 0, 0, tiled=True)
    return last_pass(parts, table), log_norm[0]


def solution(mesh):
    torus = Mesh(mesh.devices.reshape(4, 8, 2, 4, 2), (*AXES, *CEN))
    in_specs = (P(AXES, None), P(CEN, None))
    out_specs = (P((*CEN, *AXES), None), P(AXES))
    return jax.shard_map(body, mesh=torus, in_specs=in_specs, out_specs=out_specs, check_vma=False)
```

```python
import jax
import jax.numpy as jnp
from jax import lax
from jax.experimental import pallas as pl
from jax.experimental.pallas import tpu as pltpu
from jax.sharding import Mesh
from jax.sharding import PartitionSpec as P

AXES = ("yl", "z", "co")
CEN = ("x", "yh")
GATHER = ("yl", "co")
REDUCE = "z"
RING = ("yl", "co", "yh")
MIB = 1 << 20
ORDER = (7, 6, 5, 4, 3, 2, 1, 0)
CHUNK = 2048
inv_temp = 0.0625
SPAN, FLOOR = 240.0, 120.0


def squares(table):
    wide = table.astype(jnp.float32)
    return jnp.sum(wide * wide, axis=1, keepdims=True) * inv_temp


def columns(rows):
    return (rows * jnp.bfloat16(2.0 * inv_temp)).T


def products(table, columns):
    return jnp.dot(table, columns, preferred_element_type=jnp.float32)


def first_kernel(centroids, points, stats, reduced, table, rows, turned, arrived, ready):
    pieces = (slice(0, CHUNK), slice(CHUNK, table.shape[0]))
    own = pltpu.make_async_copy(points, rows, ready)
    copies = [
        pltpu.make_async_copy(centroids.at[piece], table.at[piece], arrived.at[i])
        for i, piece in enumerate(pieces)
    ]
    own.start()
    for copy in copies:
        copy.start()
    own.wait()
    turned[...] = columns(rows[...])

    found = []
    for copy, piece in zip(copies, pieces):
        copy.wait()
        block = table[piece, :]
        logits = products(block, turned[...]) - squares(block)
        top = jnp.max(logits, axis=0, keepdims=True)
        found.append((top, jnp.sum(jnp.exp(logits - top), axis=0, keepdims=True)))
    peak = jnp.maximum(found[0][0], found[1][0])
    total = sum(part * jnp.exp(top - peak) for top, part in found)
    both = jnp.concatenate([peak, total], axis=0)
    for i in range(stats.shape[0]):
        stats[i] = both
    yl, co = (lax.axis_index(a) for a in GATHER)
    count, owned, _ = reduced.shape
    for z in range(count):
        at = ((yl * count + ORDER[z]) * lax.axis_size("co") + co) * owned
        reduced[z] = table[pl.ds(pl.multiple_of(at, owned), owned), :]


def first_pass(points, centroids, receivers, reduced, owned):
    n, d = points.shape
    k = centroids.shape[0]
    return pl.pallas_call(
        first_kernel,
        in_specs=[pl.BlockSpec(memory_space=pltpu.HBM)] * 2,
        out_specs=[pl.BlockSpec(memory_space=pltpu.VMEM)] * 2,
        out_shape=[
            jax.ShapeDtypeStruct((receivers, 2, n), jnp.float32),
            jax.ShapeDtypeStruct((reduced, owned, d), centroids.dtype),
        ],
        scratch_shapes=[
            pltpu.VMEM((k, d), centroids.dtype),
            pltpu.VMEM((n, d), points.dtype),
            pltpu.VMEM((d, n), points.dtype),
            pltpu.SemaphoreType.DMA((2,)),
            pltpu.SemaphoreType.DMA,
        ],
        compiler_params=pltpu.CompilerParams(vmem_limit_bytes=32 * MIB),
        cost_estimate=pl.CostEstimate(
            flops=2 * n * k * d, bytes_accessed=2 * k * d, transcendentals=n * k
        ),
        name="first_pass",
    )(*(pltpu.with_memory_space_constraint(a, pltpu.HBM) for a in (centroids, points)))


def second_kernel(stats, table, near, sides, far, parts, own_norm, log_norms, sums, masses):
    yl, co = (lax.axis_index(a) for a in GATHER)

    cen = stats.shape[0]
    peak = stats[0, :, 0, :]
    for c in range(1, cen):
        peak = jnp.maximum(peak, stats[c, :, 0, :])
    total = stats[0, :, 1, :] * jnp.exp(stats[0, :, 0, :] - peak)
    for c in range(1, cen):
        total = total + stats[c, :, 1, :] * jnp.exp(stats[c, :, 0, :] - peak)
    log_norms[...] = peak + jnp.log(total)
    own_norm[...] = log_norms[pl.ds(7 - yl * 2 - co, 1), :]

    norms = squares(table[...])
    cores, n, d = near.shape
    groups = ((near, (0,)), (sides, (3, 1)), (far, (2,)))
    for rows, offs in groups:
        chips = [lax.rem(yl + off, 4) * cores for off in offs]
        shift = [log_norms[pl.ds(7 - chip - c, 1), :] for chip in chips for c in range(cores)]
        count = len(shift) * n
        points = rows[...].reshape(count, d)
        logits = products(table[...], columns(points)) - norms
        shares = jnp.exp(logits - jnp.concatenate(shift, axis=1)).astype(jnp.bfloat16)
        product = jnp.dot(shares, points, preferred_element_type=jnp.float32)
        wide = shares.astype(jnp.float32)
        mass = sum(wide[:, i : i + 128] for i in range(0, count, 128))
        if rows is near:
            sums[...] = product
            masses[...] = mass
        else:
            sums[...] += product
            masses[...] += mass

    owned = sums.shape[0] // parts.shape[0]
    line = lax.broadcasted_iota(jnp.int32, (16, 128), 0)
    for r in range(parts.shape[0]):
        here = slice(r * owned, (r + 1) * owned)
        mass = masses[here, :]
        mean = sums[here, :] / (1.0 + jnp.sum(mass, axis=1, keepdims=True))
        size = jnp.abs(mean)
        scale = jnp.maximum(jnp.max(size, axis=0, keepdims=True) * 1.01, 1e-30)
        scale = scale.astype(jnp.bfloat16).astype(jnp.float32)
        code = jnp.exp2(size * (SPAN / scale) - FLOOR)
        code = jnp.where(mean < 0.0, -code, code).astype(jnp.bfloat16)
        parts[r, :owned, :] = code[:, :128]
        parts[r, owned : 2 * owned, :] = code[:, 128:]
        mass = jnp.sum(mass.T, axis=0, keepdims=True)
        high = mass.astype(jnp.bfloat16).astype(jnp.float32)
        mid = (mass - high).astype(jnp.bfloat16).astype(jnp.float32)
        tail = mass - high - mid
        for at, row in enumerate((scale[:, :128], scale[:, 128:], high, mid)):
            tail = jnp.where(line == at, row, tail)
        parts[r, 2 * owned :, :] = tail.astype(jnp.bfloat16)


def second_pass(stats, table, blocks):
    reduced, owned, d = table.shape
    g, n = stats.shape[1], stats.shape[3]
    k = owned * reduced
    return pl.pallas_call(
        second_kernel,
        in_specs=[pl.BlockSpec(memory_space=pltpu.VMEM)] * 5,
        out_specs=[pl.BlockSpec(memory_space=pltpu.VMEM)] * 2,
        out_shape=[
            jax.ShapeDtypeStruct((reduced, 2 * owned + 16, d // 2), jnp.bfloat16),
            jax.ShapeDtypeStruct((1, n), jnp.float32),
        ],
        scratch_shapes=[
            pltpu.VMEM((g, n), jnp.float32),
            pltpu.VMEM((k, d), jnp.float32),
            pltpu.VMEM((k, 128), jnp.float32),
        ],
        compiler_params=pltpu.CompilerParams(vmem_limit_bytes=24 * MIB),
        cost_estimate=pl.CostEstimate(
            flops=4 * g * n * k * d, bytes_accessed=4 * k * d, transcendentals=g * n * k
        ),
        name="second_pass",
    )(stats, table.reshape(k, d), *blocks)


def last_kernel(parts, table, updated):
    owned = updated.shape[0]
    z = lax.axis_index(REDUCE)
    own = table[sum(jnp.where(z == at, r, 0) for r, at in enumerate(ORDER))]
    sums = own.astype(jnp.float32)
    masses = jnp.ones((owned, owned), jnp.float32)
    for r in range(parts.shape[0]):
        tail = parts[r, 2 * owned :, :].astype(jnp.float32)
        mass = jnp.broadcast_to(tail[2:3] + tail[3:4] + tail[4:5], (owned, owned)).T
        means = []
        for half in range(2):
            code = parts[r, half * owned : (half + 1) * owned, :].astype(jnp.float32)
            size = (jnp.log2(jnp.abs(code)) + FLOOR) * (tail[half : half + 1] / SPAN)
            means.append(jnp.where(code < 0.0, -size, size) * (1.0 + mass))
        sums = sums + jnp.concatenate(means, axis=1)
        masses = masses + mass
    updated[...] = sums / jnp.concatenate([masses, masses], axis=1)


def last_pass(parts, table):
    reduced, owned, d = table.shape
    return pl.pallas_call(
        last_kernel,
        in_specs=[pl.BlockSpec(memory_space=pltpu.VMEM)] * 2,
        out_specs=pl.BlockSpec(memory_space=pltpu.VMEM),
        out_shape=jax.ShapeDtypeStruct((owned, d), jnp.float32),
        compiler_params=pltpu.CompilerParams(vmem_limit_bytes=16 * MIB),
        name="last_pass",
    )(parts, table)


def moved(array, hops):
    low, cores, high = (lax.axis_size(a) for a in RING)
    ring = low * high

    def place(y, core):
        return ((y % low) * cores + core) * high + y // low

    pairs = [
        (place(y, core), place((y + hops[core]) % ring, core))
        for y in range(ring)
        for core in range(cores)
    ]
    return lax.ppermute(array, RING, pairs)


def body(points, centroids):
    n, d = points.shape
    cen = lax.axis_size(CEN)
    gathered = lax.axis_size(GATHER)
    reduced = lax.axis_size(REDUCE)
    owned = centroids.shape[0] // (gathered * reduced)

    near = lax.all_gather(points, "co")
    side, far = moved(near, (1, -1)), moved(near, (2, -2))
    stats, table = first_pass(points, centroids, cen * gathered, reduced, owned)
    side, _ = lax.optimization_barrier((side, stats))
    sides = lax.all_gather(side, "co")
    turned = [list(range(cen * gathered))[::-1]]
    every = lax.all_to_all(
        stats, (*CEN, *GATHER), 0, 0, tiled=True, axis_index_groups=turned
    )
    every = every.reshape(cen, gathered, 2, n)
    parts, log_norm = second_pass(every, table, (near, sides, far))
    parts = lax.all_to_all(parts, REDUCE, 0, 0, tiled=True, axis_index_groups=[list(ORDER)])
    return last_pass(parts, table), log_norm[0]


def solution(mesh):
    torus = Mesh(mesh.devices.reshape(4, 8, 2, 4, 2), (*AXES, *CEN))
    in_specs = (P(AXES, None), P(CEN, None))
    out_specs = (P((*CEN, *AXES), None), P(AXES))
    return jax.shard_map(body, mesh=torus, in_specs=in_specs, out_specs=out_specs, check_vma=False)
```

```python
import jax
import jax.numpy as jnp
from jax import lax
from jax.experimental import pallas as pl
from jax.experimental.pallas import tpu as pltpu
from jax.sharding import Mesh
from jax.sharding import PartitionSpec as P

AXES = ("yl", "z", "co")
CEN = ("x", "yh")
GATHER = ("yl", "co")
REDUCE = "z"
RING = ("yl", "co", "yh")
MIB = 1 << 20
ORDER = (7, 3, 6, 2, 5, 1, 4, 0)
CHUNK = 2048
inv_temp = 0.0625
SPAN, FLOOR = 240.0, 120.0


def squares(table):
    wide = table.astype(jnp.float32)
    return jnp.sum(wide * wide, axis=1, keepdims=True) * inv_temp


def columns(rows):
    return (rows * jnp.bfloat16(2.0 * inv_temp)).T


def products(table, columns):
    return jnp.dot(table, columns, preferred_element_type=jnp.float32)


def first_kernel(centroids, points, stats, reduced, table, rows, turned, arrived, ready):
    pieces = (slice(0, CHUNK), slice(CHUNK, table.shape[0]))
    own = pltpu.make_async_copy(points, rows, ready)
    copies = [
        pltpu.make_async_copy(centroids.at[piece], table.at[piece], arrived.at[i])
        for i, piece in enumerate(pieces)
    ]
    own.start()
    for copy in copies:
        copy.start()
    own.wait()
    turned[...] = columns(rows[...])

    found = []
    for copy, piece in zip(copies, pieces):
        copy.wait()
        block = table[piece, :]
        logits = products(block, turned[...]) - squares(block)
        top = jnp.max(logits, axis=0, keepdims=True)
        found.append((top, jnp.sum(jnp.exp(logits - top), axis=0, keepdims=True)))
    peak = jnp.maximum(found[0][0], found[1][0])
    total = sum(part * jnp.exp(top - peak) for top, part in found)
    both = jnp.concatenate([peak, total], axis=0)
    for i in range(stats.shape[0]):
        stats[i] = both
    yl, co = (lax.axis_index(a) for a in GATHER)
    count, owned, _ = reduced.shape
    for z in range(count):
        at = ((yl * count + ORDER[z]) * lax.axis_size("co") + co) * owned
        reduced[z] = table[pl.ds(pl.multiple_of(at, owned), owned), :]


def first_pass(points, centroids, receivers, reduced, owned):
    n, d = points.shape
    k = centroids.shape[0]
    return pl.pallas_call(
        first_kernel,
        in_specs=[pl.BlockSpec(memory_space=pltpu.HBM)] * 2,
        out_specs=[pl.BlockSpec(memory_space=pltpu.VMEM)] * 2,
        out_shape=[
            jax.ShapeDtypeStruct((receivers, 2, n), jnp.float32),
            jax.ShapeDtypeStruct((reduced, owned, d), centroids.dtype),
        ],
        scratch_shapes=[
            pltpu.VMEM((k, d), centroids.dtype),
            pltpu.VMEM((n, d), points.dtype),
            pltpu.VMEM((d, n), points.dtype),
            pltpu.SemaphoreType.DMA((2,)),
            pltpu.SemaphoreType.DMA,
        ],
        compiler_params=pltpu.CompilerParams(vmem_limit_bytes=32 * MIB),
        cost_estimate=pl.CostEstimate(
            flops=2 * n * k * d, bytes_accessed=2 * k * d, transcendentals=n * k
        ),
        name="first_pass",
    )(*(pltpu.with_memory_space_constraint(a, pltpu.HBM) for a in (centroids, points)))


def second_kernel(stats, table, near, sides, far, parts, own_norm, log_norms, sums, masses):
    yl, co = (lax.axis_index(a) for a in GATHER)

    cen = stats.shape[0]
    peak = stats[0, :, 0, :]
    for c in range(1, cen):
        peak = jnp.maximum(peak, stats[c, :, 0, :])
    total = stats[0, :, 1, :] * jnp.exp(stats[0, :, 0, :] - peak)
    for c in range(1, cen):
        total = total + stats[c, :, 1, :] * jnp.exp(stats[c, :, 0, :] - peak)
    log_norms[...] = peak + jnp.log(total)
    own_norm[...] = log_norms[pl.ds(7 - yl * 2 - co, 1), :]

    norms = squares(table[...])
    cores, n, d = near.shape
    groups = ((near, (0,)), (sides, (3, 1)), (far, (2,)))
    for rows, offs in groups:
        chips = [lax.rem(yl + off, 4) * cores for off in offs]
        shift = [log_norms[pl.ds(7 - chip - c, 1), :] for chip in chips for c in range(cores)]
        count = len(shift) * n
        points = rows[...].reshape(count, d)
        logits = products(table[...], columns(points)) - norms
        shares = jnp.exp(logits - jnp.concatenate(shift, axis=1)).astype(jnp.bfloat16)
        product = jnp.dot(shares, points, preferred_element_type=jnp.float32)
        wide = shares.astype(jnp.float32)
        mass = sum(wide[:, i : i + 128] for i in range(0, count, 128))
        if rows is near:
            sums[...] = product
            masses[...] = mass
        else:
            sums[...] += product
            masses[...] += mass

    owned = sums.shape[0] // parts.shape[0]
    line = lax.broadcasted_iota(jnp.int32, (16, 128), 0)
    for r in range(parts.shape[0]):
        here = slice(r * owned, (r + 1) * owned)
        mass = masses[here, :]
        mean = sums[here, :] / (1.0 + jnp.sum(mass, axis=1, keepdims=True))
        size = jnp.abs(mean)
        scale = jnp.maximum(jnp.max(size, axis=0, keepdims=True) * 1.01, 1e-30)
        scale = scale.astype(jnp.bfloat16).astype(jnp.float32)
        code = jnp.exp2(size * (SPAN / scale) - FLOOR)
        code = jnp.where(mean < 0.0, -code, code).astype(jnp.bfloat16)
        parts[r, :owned, :] = code[:, :128]
        parts[r, owned : 2 * owned, :] = code[:, 128:]
        mass = jnp.sum(mass.T, axis=0, keepdims=True)
        high = mass.astype(jnp.bfloat16).astype(jnp.float32)
        mid = (mass - high).astype(jnp.bfloat16).astype(jnp.float32)
        tail = mass - high - mid
        for at, row in enumerate((scale[:, :128], scale[:, 128:], high, mid)):
            tail = jnp.where(line == at, row, tail)
        parts[r, 2 * owned :, :] = tail.astype(jnp.bfloat16)


def second_pass(stats, table, blocks):
    reduced, owned, d = table.shape
    g, n = stats.shape[1], stats.shape[3]
    k = owned * reduced
    return pl.pallas_call(
        second_kernel,
        in_specs=[pl.BlockSpec(memory_space=pltpu.VMEM)] * 5,
        out_specs=[pl.BlockSpec(memory_space=pltpu.VMEM)] * 2,
        out_shape=[
            jax.ShapeDtypeStruct((reduced, 2 * owned + 16, d // 2), jnp.bfloat16),
            jax.ShapeDtypeStruct((1, n), jnp.float32),
        ],
        scratch_shapes=[
            pltpu.VMEM((g, n), jnp.float32),
            pltpu.VMEM((k, d), jnp.float32),
            pltpu.VMEM((k, 128), jnp.float32),
        ],
        compiler_params=pltpu.CompilerParams(vmem_limit_bytes=24 * MIB),
        cost_estimate=pl.CostEstimate(
            flops=4 * g * n * k * d, bytes_accessed=4 * k * d, transcendentals=g * n * k
        ),
        name="second_pass",
    )(stats, table.reshape(k, d), *blocks)


def last_kernel(parts, table, updated):
    owned = updated.shape[0]
    z = lax.axis_index(REDUCE)
    own = table[sum(jnp.where(z == at, r, 0) for r, at in enumerate(ORDER))]
    sums = own.astype(jnp.float32)
    masses = jnp.ones((owned, owned), jnp.float32)
    for r in range(parts.shape[0]):
        tail = parts[r, 2 * owned :, :].astype(jnp.float32)
        mass = jnp.broadcast_to(tail[2:3] + tail[3:4] + tail[4:5], (owned, owned)).T
        means = []
        for half in range(2):
            code = parts[r, half * owned : (half + 1) * owned, :].astype(jnp.float32)
            size = (jnp.log2(jnp.abs(code)) + FLOOR) * (tail[half : half + 1] / SPAN)
            means.append(jnp.where(code < 0.0, -size, size) * (1.0 + mass))
        sums = sums + jnp.concatenate(means, axis=1)
        masses = masses + mass
    updated[...] = sums / jnp.concatenate([masses, masses], axis=1)


def last_pass(parts, table):
    reduced, owned, d = table.shape
    return pl.pallas_call(
        last_kernel,
        in_specs=[pl.BlockSpec(memory_space=pltpu.VMEM)] * 2,
        out_specs=pl.BlockSpec(memory_space=pltpu.VMEM),
        out_shape=jax.ShapeDtypeStruct((owned, d), jnp.float32),
        compiler_params=pltpu.CompilerParams(vmem_limit_bytes=16 * MIB),
        name="last_pass",
    )(parts, table)


def moved(array, hops):
    low, cores, high = (lax.axis_size(a) for a in RING)
    ring = low * high

    def place(y, core):
        return ((y % low) * cores + core) * high + y // low

    pairs = [
        (place(y, core), place((y + hops[core]) % ring, core))
        for y in range(ring)
        for core in range(cores)
    ]
    return lax.ppermute(array, RING, pairs)


def body(points, centroids):
    n, d = points.shape
    cen = lax.axis_size(CEN)
    gathered = lax.axis_size(GATHER)
    reduced = lax.axis_size(REDUCE)
    owned = centroids.shape[0] // (gathered * reduced)

    near = lax.all_gather(points, "co")
    side, far = moved(near, (1, -1)), moved(near, (2, -2))
    stats, table = first_pass(points, centroids, cen * gathered, reduced, owned)
    side, _ = lax.optimization_barrier((side, stats))
    sides = lax.all_gather(side, "co")
    turned = [list(range(cen * gathered))[::-1]]
    every = lax.all_to_all(
        stats, (*CEN, *GATHER), 0, 0, tiled=True, axis_index_groups=turned
    )
    every = every.reshape(cen, gathered, 2, n)
    parts, log_norm = second_pass(every, table, (near, sides, far))
    parts = lax.all_to_all(parts, REDUCE, 0, 0, tiled=True, axis_index_groups=[list(ORDER)])
    return last_pass(parts, table), log_norm[0]


def solution(mesh):
    torus = Mesh(mesh.devices.reshape(4, 8, 2, 4, 2), (*AXES, *CEN))
    in_specs = (P(AXES, None), P(CEN, None))
    out_specs = (P((*CEN, *AXES), None), P(AXES))
    return jax.shard_map(body, mesh=torus, in_specs=in_specs, out_specs=out_specs, check_vma=False)
```
